32 devices in a mesh: parts: 2 (over y), chan: 4 (over z), tm: 2 (over x), rep: 2 (over core).
Axes of the slice: x: 2, y: 2, z: 4, core: 2. Of those that a mesh axis runs over, the one named last changes fastest.
Arguments:
- records: bfloat16 [64, 512, 512], P(('chan', 'tm', 'rep'), 'parts'), parts along dimension 1, may hold values from -6 to 6
- fir_taps: float32 [65], replicated, may hold values from -0.75 to 0.75
- source_ids: int32 [8], P('parts'), parts along dimension 0, may hold values from 0 to 3
Outputs:
- correlations: float32 [4, 512, 256], P(None, ('parts', 'chan')), parts along dimension 1
The draws below stay inside these ranges and needn't reach their ends.
There are 2 independent parts, one for each index of `parts`. The reference program is written for one: setup_inputs(seed, part) draws one part's arguments, and reference() takes and returns one part's arrays. A program takes and returns all parts, laid end to end along the dimension named above; an argument that names none is the same for every part. Nothing has to cross between parts.
Inputs may be any that keep to these rules, and one draw needn't show every extreme that they name: `source_ids`: block indices along the segment, repeats allowed.
All inputs are finite; a program needn't handle non-finite values.
Results may differ from the reference program's by a relative error of at most 0.0074.
Values may be sent and summed in bfloat16 or wider, within the bound.
No kernel may reach another device: no remote copies, remote signals or barrier semaphores. Data moves between devices by JAX's collectives and lax.ppermute only.
A program may use at most 64 MiB of HBM per device.

```python
import math
from functools import partial
import jax
import jax.numpy as jnp
from jax import lax

BLOCK = 64
SAMP = 512
BINS = 96
LAGS = 256
TAPS = 65
SRCB = 4
WINDOWS = 64
BLOCKS = 4
CHANNELS = 256


def with_ends(values, stream_key, smallest, top_value):
    extent = values.shape
    index_at = [jax.random.randint(jax.random.fold_in(stream_key, axis), (), 0, extent[axis]) for axis in range(len(extent))]
    values = values.at[tuple(index_at)].set(smallest)
    longest = extent.index(max(extent))
    index_at[longest] = (index_at[longest] + 1) % extent[longest]
    return values.at[tuple(index_at)].set(top_value)


def levels(own_key, dims, split, low, high):
    gain = 1.0
    for position, shards_of in split:
        heights = jax.random.uniform(jax.random.fold_in(jax.random.fold_in(own_key, 6), position), (shards_of,), jnp.float32, low / len(split), high / len(split))
        gain = gain * jnp.repeat(jnp.exp(heights), dims[position] // shards_of).reshape((-1,) + (1,) * (len(dims) - 1 - position))
    return gain


def scatter_about(stream_key, shape, spread, reach, pieces=(), held_as=jnp.bfloat16):
    entries = jax.random.normal(stream_key, shape, jnp.float32) * spread
    if len(pieces) > 0:
        entries = levels(stream_key, shape, pieces, -0.22, 0.18) * entries
    return jnp.clip(entries, min=-reach, max=reach).astype(held_as)


def setup_inputs(seed: int = 0, part: int = 0) -> dict:
    streams_of = jax.random.split(jax.random.key(seed), 4)
    part_keys = jax.random.split(jax.random.fold_in(streams_of[3], part), 4)
    records = scatter_about(part_keys[0], (WINDOWS, CHANNELS, SAMP), 1.0, 6.0, ((0, 16),))
    fir_taps = scatter_about(streams_of[1], (TAPS,), TAPS ** -0.5, 0.75, (), jnp.float32)
    source_ids = with_ends(jax.random.randint(part_keys[2], (SRCB,), 0, BLOCKS), jax.random.fold_in(part_keys[2], 1), 0, BLOCKS - 1).astype(jnp.int32)
    return dict(records=records, fir_taps=fir_taps, source_ids=source_ids)


def fir_matrix(fir_taps, samples):
    taps = fir_taps.shape[0]
    half = taps // 2
    rows = jnp.arange(samples)[:, None]
    cols = jnp.arange(samples)[None, :]
    offset = rows - cols + half
    inside = (offset >= 0) & (offset < taps)
    values = jnp.take(fir_taps, jnp.clip(offset, 0, taps - 1))
    return jnp.where(inside, values, jnp.float32(0.0)).astype(jnp.bfloat16)

def dft_table(samples, bins):
    times = jnp.arange(samples)[:, None]
    freqs = jnp.arange(1, bins + 1)[None, :]
    angle = 2.0 * math.pi / samples * (times * freqs % samples).astype(jnp.float32)
    return jnp.concatenate([jnp.cos(angle), -jnp.sin(angle)], axis=1).astype(jnp.bfloat16)

def lag_table(samples, bins, lags):
    freqs = jnp.arange(1, bins + 1)[:, None]
    shifts = jnp.arange(lags)[None, :] - lags // 2
    angle = 2.0 * math.pi / samples * jnp.mod(freqs * shifts, samples).astype(jnp.float32)
    return jnp.concatenate([jnp.cos(angle), -jnp.sin(angle)], axis=0)

def whiten(block, fir, dft):
    highest = lax.Precision.HIGHEST
    filtered = jnp.einsum('wcs,st->wct', block.astype(jnp.float32), fir.astype(jnp.float32), precision=highest).astype(jnp.bfloat16)
    spectra = jnp.einsum('wct,tf->wcf', filtered.astype(jnp.float32), dft.astype(jnp.float32), precision=highest)
    real_part = spectra[..., :BINS]
    imag_part = spectra[..., BINS:]
    amp = jnp.sqrt(real_part * real_part + imag_part * imag_part)
    padded = jnp.pad(amp, ((0, 0), (0, 0), (2, 2)))
    smooth = (padded[..., 0:BINS] + padded[..., 1:BINS + 1] + padded[..., 2:BINS + 2] + padded[..., 3:BINS + 3] + padded[..., 4:BINS + 4]) / 5.0
    mean_amp = lax.optimization_barrier(jnp.mean(amp, axis=-1, keepdims=True)) + 1e-06
    level = jnp.maximum(smooth, 0.5 * mean_amp)
    return (spectra / jnp.concatenate([level, level], axis=-1)).astype(jnp.bfloat16)

def reference(records, fir_taps, source_ids):
    windows, channels, samples = records.shape
    blocks = channels // BLOCK
    fir = fir_matrix(fir_taps, samples)
    dft = dft_table(samples, BINS)
    table = lag_table(samples, BINS, LAGS)
    grouped = jnp.transpose(records.reshape(windows, blocks, BLOCK, samples), (1, 0, 2, 3))
    white = lax.map(lambda blk: whiten(blk, fir, dft), grouped)
    chosen = jnp.take(white, source_ids.astype(jnp.int32), axis=0)
    source = lax.optimization_barrier(jnp.sum(chosen.astype(jnp.float32), axis=2))
    white_re = white[..., :BINS].astype(jnp.float32)
    white_im = white[..., BINS:].astype(jnp.float32)
    src_re = source[..., :BINS]
    src_im = source[..., BINS:]
    product = partial(jnp.einsum, precision=lax.Precision.HIGHEST)
    cross_re = product('bwif,swf->sbif', white_re, src_re) + product('bwif,swf->sbif', white_im, src_im)
    cross_im = product('bwif,swf->sbif', white_im, src_re) - product('bwif,swf->sbif', white_re, src_im)
    cross = jnp.concatenate([cross_re, cross_im], axis=-1).reshape(SRCB, channels, 2 * BINS)
    scale = 1.0 / math.sqrt(windows * BLOCK * BINS)
    return scale * jnp.einsum('scf,fl->scl', cross, table, precision=lax.Precision.HIGHEST)
```

```python
import functools
import math

import jax
import jax.numpy as jnp
import numpy as np
from jax import lax
from jax.experimental import pallas as pl
from jax.experimental.pallas import tpu as pltpu
from jax.sharding import PartitionSpec as P

BINS = 96
LAGS = 256
BLOCK = 64
LANES = 128
VMEM_LIMIT = 32 * 1024 * 1024


def dft_table(samples):
    times = np.arange(samples)[:, None]
    freqs = np.arange(1, BINS + 1)[None, :]
    angle = np.float32(2.0 * math.pi / samples) * (times * freqs % samples).astype(np.float32)
    table = np.zeros((samples, 2 * LANES), np.float32)
    table[:, :BINS] = np.cos(angle)
    table[:, LANES : LANES + BINS] = -np.sin(angle)
    return table.astype(jnp.bfloat16)


def lag_table(samples):
    freqs = np.arange(1, BINS + 1)[:, None]
    shifts = np.arange(LAGS)[None, :] - LAGS // 2
    angle = np.float32(2.0 * math.pi / samples) * np.mod(freqs * shifts, samples).astype(np.float32)
    table = np.zeros((2 * LANES, LAGS), np.float32)
    table[:BINS] = np.cos(angle)
    table[LANES : LANES + BINS] = -np.sin(angle)
    high = table.astype(jnp.bfloat16)
    low = (table - high.astype(np.float32)).astype(jnp.bfloat16)
    return np.concatenate([high, low], axis=0)


def fir_blocks(taps_ref, pad_ref):
    taps = taps_ref.shape[1]
    half = taps // 2
    pad_ref[...] = jnp.zeros(pad_ref.shape, jnp.float32)
    pad_ref[0:1, 0:taps] = taps_ref[...]
    rows = lax.broadcasted_iota(jnp.int32, (LANES, LANES), 0)
    cols = lax.broadcasted_iota(jnp.int32, (LANES, LANES), 1)
    flip = (rows + cols == taps - 1).astype(jnp.bfloat16)
    turned = jnp.dot(
        pad_ref[...].astype(jnp.bfloat16), flip, preferred_element_type=jnp.float32
    )[0:1]
    wide = jnp.concatenate([turned, jnp.zeros((1, 2 * LANES), jnp.float32)], axis=1)
    wide = jnp.broadcast_to(wide, (LANES, 3 * LANES))
    return pltpu.roll(wide, LANES - half, 1, stride=1, stride_axis=0)


def pack(re, im):
    lane = lax.broadcasted_iota(jnp.int32, re[0].shape, 1)
    tiles = []
    for index in range(3):
        for part, last in ((re[index], re[3]), (im[index], im[3])):
            moved = pltpu.roll(last, BINS - 32 * index, 1)
            tiles.append(jnp.where(lane < BINS, part, moved))
    return jnp.concatenate(tiles, axis=1)


def unpack(packed):
    lane = lax.broadcasted_iota(jnp.int32, (packed.shape[0], LANES), 1)
    tiles = [packed[:, LANES * i : LANES * (i + 1)] for i in range(6)]
    last = []
    for which in range(2):
        total = jnp.zeros_like(tiles[0])
        for index in range(3):
            moved = pltpu.roll(tiles[2 * index + which], LANES - BINS + 32 * index, 1)
            total = jnp.where((lane >= 32 * index) & (lane < 32 * index + 32), moved, total)
        last.append(total)
    rows = [jnp.concatenate([tiles[2 * i], tiles[2 * i + 1]], axis=1) for i in range(3)]
    return jnp.concatenate(rows + [jnp.concatenate(last, axis=1)], axis=0)


def spectra_kernel(me_ref, ids_ref, rec_ref, taps_ref, dft_ref, out_ref, pad, fir, white, sums):
    windows, channels, samples = rec_ref.shape
    blocks = channels // BLOCK
    count = ids_ref.shape[0]
    three = fir_blocks(taps_ref, pad).astype(jnp.bfloat16)
    fir[...] = jnp.zeros(fir.shape, fir.dtype)
    tiles = samples // LANES
    for i in range(tiles):
        for j in range(max(i - 1, 0), min(i + 2, tiles)):
            fir[LANES * i : LANES * (i + 1), LANES * j : LANES * (j + 1)] = three[
                :, LANES * (j - i + 1) : LANES * (j - i + 2)
            ]
    for b in range(blocks):
        rows = rec_ref[:, BLOCK * b : BLOCK * (b + 1), :].reshape(windows * BLOCK, samples)
        filtered = jnp.dot(rows, fir[...], preferred_element_type=jnp.float32).astype(jnp.bfloat16)
        spectra = jnp.dot(filtered, dft_ref[...], preferred_element_type=jnp.float32)
        re, im = spectra[:, :LANES], spectra[:, LANES:]
        amp = jnp.sqrt(re * re + im * im)
        pair = amp + pltpu.roll(amp, 1, 1)
        smooth = (pltpu.roll(pair, LANES - 2, 1) + pair + pltpu.roll(amp, 2, 1)) / 5.0
        mean_amp = jnp.sum(amp, axis=1, keepdims=True) / BINS + 1e-06
        level = jnp.maximum(smooth, 0.5 * mean_amp)
        scale = 1.0 / level
        for which, value in enumerate((re, im)):
            unit = (value * scale).astype(jnp.bfloat16)
            white[which, b] = unit.reshape(windows, BLOCK, LANES)
            sums[which, b] = jnp.sum(
                unit.astype(jnp.float32).reshape(windows, BLOCK, LANES), axis=1
            )
    for k in range(blocks):
        b = lax.rem(me_ref[0] + k, blocks)
        re, im = [], []
        for s in range(count):
            total_re = jnp.zeros((BLOCK, LANES), jnp.float32)
            total_im = jnp.zeros((BLOCK, LANES), jnp.float32)
            for w in range(windows):
                src_re = sums[0, ids_ref[s], w : w + 1, :]
                src_im = sums[1, ids_ref[s], w : w + 1, :]
                white_re = white[0, b, w].astype(jnp.float32)
                white_im = white[1, b, w].astype(jnp.float32)
                total_re += white_re * src_re + white_im * src_im
                total_im += white_im * src_re - white_re * src_im
            re.append(total_re)
            im.append(total_im)
        out_ref[BLOCK * k : BLOCK * (k + 1), :] = pack(re, im).astype(jnp.bfloat16)


def local_cross(me, source_ids, records, taps, dft):
    windows, channels, samples = records.shape
    blocks = channels // BLOCK
    vmem = pl.BlockSpec(memory_space=pltpu.VMEM)
    smem = pl.BlockSpec(memory_space=pltpu.SMEM)
    return pl.pallas_call(
        spectra_kernel,
        out_shape=jax.ShapeDtypeStruct((channels, 6 * LANES), jnp.bfloat16),
        in_specs=[smem, smem, vmem, vmem, vmem],
        out_specs=vmem,
        scratch_shapes=[
            pltpu.VMEM((8, LANES), jnp.float32),
            pltpu.VMEM((samples, samples), jnp.bfloat16),
            pltpu.VMEM((2, blocks, windows, BLOCK, LANES), jnp.bfloat16),
            pltpu.VMEM((2, blocks, windows, LANES), jnp.float32),
        ],
        compiler_params=pltpu.CompilerParams(vmem_limit_bytes=VMEM_LIMIT),
    )(me, source_ids, records, taps, dft)


def add_kernel(pieces, *refs):
    inputs, outputs = refs[: len(refs) - pieces], refs[len(refs) - pieces :]
    rows = outputs[0].shape[0]
    for k, out in enumerate(outputs):
        at = slice(rows * k, rows * (k + 1))
        total = inputs[0][at, :].astype(jnp.float32)
        for ref in inputs[1:]:
            total += ref[at, :].astype(jnp.float32)
        out[...] = total.astype(out.dtype)


def added(arrays, pieces):
    rows, width = arrays[0].shape
    vmem = pl.BlockSpec(memory_space=pltpu.VMEM)
    return pl.pallas_call(
        functools.partial(add_kernel, pieces),
        out_shape=[jax.ShapeDtypeStruct((rows // pieces, width), jnp.bfloat16)] * pieces,
        in_specs=[vmem] * len(arrays),
        out_specs=[vmem] * pieces,
        compiler_params=pltpu.CompilerParams(vmem_limit_bytes=VMEM_LIMIT),
    )(*arrays)


def gather_kernel(core_ref, *refs):
    own, first, rest, out = refs[0], refs[1], refs[2:-1], refs[-1]
    total = jnp.where(core_ref[0] == 0, own[...].astype(jnp.float32), first[...].astype(jnp.float32))
    for ref in rest:
        total += ref[...].astype(jnp.float32)
    out[...] = total.astype(out.dtype)


def gathered(core, arrays):
    vmem = pl.BlockSpec(memory_space=pltpu.VMEM)
    smem = pl.BlockSpec(memory_space=pltpu.SMEM)
    return pl.pallas_call(
        gather_kernel,
        out_shape=jax.ShapeDtypeStruct(arrays[0].shape, jnp.bfloat16),
        in_specs=[smem] + [vmem] * len(arrays),
        out_specs=vmem,
        compiler_params=pltpu.CompilerParams(vmem_limit_bytes=VMEM_LIMIT),
    )(core, *arrays)


def lag_kernel(scale, table_ref, *refs):
    out = refs[-1]
    total = refs[0][...].astype(jnp.float32)
    for ref in refs[1:-1]:
        total += ref[...].astype(jnp.float32)
    cross = unpack(total)
    high = cross.astype(jnp.bfloat16)
    low = (cross - high.astype(jnp.float32)).astype(jnp.bfloat16)
    dot = functools.partial(jnp.dot, preferred_element_type=jnp.float32)
    top, bottom = table_ref[: 2 * LANES, :], table_ref[2 * LANES :, :]
    lags = dot(high, top) + (dot(low, top) + dot(high, bottom))
    out[...] = (scale * lags).reshape(out.shape)


def to_lags(scale, table, arrays):
    vmem = pl.BlockSpec(memory_space=pltpu.VMEM)
    return pl.pallas_call(
        functools.partial(lag_kernel, scale),
        out_shape=jax.ShapeDtypeStruct((4, BLOCK, LAGS), jnp.float32),
        in_specs=[vmem] * (1 + len(arrays)),
        out_specs=vmem,
        compiler_params=pltpu.CompilerParams(vmem_limit_bytes=VMEM_LIMIT),
    )(table, *arrays)


def from_peers(value, axis):
    size = lax.axis_size(axis)
    return [
        lax.ppermute(value, axis, [(i, (i + k) % size) for i in range(size)])
        for k in range(1, size)
    ]


def body(records, fir_taps, source_ids):
    samples = records.shape[2]
    chans, times, cores = (lax.axis_size(axis) for axis in ("chan", "tm", "rep"))
    me = lax.axis_index("chan").astype(jnp.int32).reshape(1)
    core = lax.axis_index("rep").astype(jnp.int32).reshape(1)
    cross = local_cross(me, source_ids, records, fir_taps.reshape(1, -1), jnp.asarray(dft_table(samples)))
    pieces = added([cross] + from_peers(cross, "rep"), chans)
    mesh = [(a, t, r) for a in range(chans) for t in range(times) for r in range(cores)]
    place = {where: index for index, where in enumerate(mesh)}
    arrived = []
    for turn in range(-(-times // cores)):
        for k in range(chans):
            pairs = []
            for a, t, r in mesh:
                ahead = turn * cores + r
                if ahead >= times or (ahead == 0 and k == 0):
                    continue
                pairs.append((place[a, t, r], place[(a + k) % chans, (t + ahead) % times, r]))
            arrived.append(lax.ppermute(pieces[k], ("chan", "tm", "rep"), pairs))
    total = gathered(core, [pieces[0]] + arrived)
    windows_all = records.shape[0] * chans * times * cores
    scale = 1.0 / math.sqrt(windows_all * BLOCK * BINS)
    return to_lags(scale, jnp.asarray(lag_table(samples)), [total] + from_peers(total, "rep"))


def solution(mesh):
    in_specs = (P(("chan", "tm", "rep"), "parts", None), P(), P("parts"))
    out_specs = P(None, ("parts", "chan"), None)
    return jax.shard_map(body, mesh=mesh, in_specs=in_specs, out_specs=out_specs, check_vma=False)
```

```python
import functools
import math

import jax
import jax.numpy as jnp
import numpy as np
from jax import lax
from jax.experimental import pallas as pl
from jax.experimental.pallas import tpu as pltpu
from jax.sharding import PartitionSpec as P

BINS = 96
LAGS = 256
BLOCK = 64
LANES = 128
VMEM_LIMIT = 32 * 1024 * 1024


def dft_table(samples):
    times = np.arange(samples)[:, None]
    freqs = np.arange(1, BINS + 1)[None, :]
    angle = np.float32(2.0 * math.pi / samples) * (times * freqs % samples).astype(np.float32)
    table = np.zeros((samples, 2 * LANES), np.float32)
    table[:, :BINS] = np.cos(angle)
    table[:, LANES : LANES + BINS] = -np.sin(angle)
    return table.astype(jnp.bfloat16)


def lag_table(samples):
    freqs = np.arange(1, BINS + 1)[:, None]
    shifts = np.arange(LAGS)[None, :] - LAGS // 2
    angle = np.float32(2.0 * math.pi / samples) * np.mod(freqs * shifts, samples).astype(np.float32)
    table = np.zeros((2 * LANES, LAGS), np.float32)
    table[:BINS] = np.cos(angle)
    table[LANES : LANES + BINS] = -np.sin(angle)
    high = table.astype(jnp.bfloat16)
    low = (table - high.astype(np.float32)).astype(jnp.bfloat16)
    return np.concatenate([high, low], axis=0)


def fir_blocks(taps_ref, pad_ref):
    taps = taps_ref.shape[1]
    half = taps // 2
    pad_ref[...] = jnp.zeros(pad_ref.shape, jnp.float32)
    pad_ref[0:1, 0:taps] = taps_ref[...]
    rows = lax.broadcasted_iota(jnp.int32, (LANES, LANES), 0)
    cols = lax.broadcasted_iota(jnp.int32, (LANES, LANES), 1)
    flip = (rows + cols == taps - 1).astype(jnp.bfloat16)
    turned = jnp.dot(
        pad_ref[...].astype(jnp.bfloat16), flip, preferred_element_type=jnp.float32
    )[0:1]
    wide = jnp.concatenate([turned, jnp.zeros((1, 2 * LANES), jnp.float32)], axis=1)
    wide = jnp.broadcast_to(wide, (LANES, 3 * LANES))
    return pltpu.roll(wide, LANES - half, 1, stride=1, stride_axis=0)


def pack(re, im):
    lane = lax.broadcasted_iota(jnp.int32, re[0].shape, 1)
    tiles = []
    for index in range(3):
        for part, last in ((re[index], re[3]), (im[index], im[3])):
            moved = pltpu.roll(last, BINS - 32 * index, 1)
            tiles.append(jnp.where(lane < BINS, part, moved))
    return jnp.concatenate(tiles, axis=1)


def unpack(packed):
    lane = lax.broadcasted_iota(jnp.int32, (packed.shape[0], LANES), 1)
    tiles = [packed[:, LANES * i : LANES * (i + 1)] for i in range(6)]
    last = []
    for which in range(2):
        total = jnp.zeros_like(tiles[0])
        for index in range(3):
            moved = pltpu.roll(tiles[2 * index + which], LANES - BINS + 32 * index, 1)
            total = jnp.where((lane >= 32 * index) & (lane < 32 * index + 32), moved, total)
        last.append(total)
    rows = [jnp.concatenate([tiles[2 * i], tiles[2 * i + 1]], axis=1) for i in range(3)]
    return jnp.concatenate(rows + [jnp.concatenate(last, axis=1)], axis=0)


def spectra_kernel(
    me_ref,
    ids_hbm,
    rec_hbm,
    taps_hbm,
    dft_hbm,
    out_ref,
    ids_ref,
    rec_ref,
    taps_ref,
    dft_ref,
    pad,
    fir,
    white,
    sums,
    small_sems,
    dft_sem,
    rec_sems,
):
    blocks, windows, width, samples = rec_ref.shape
    count = ids_ref.shape[0]
    copies = [
        pltpu.make_async_copy(taps_hbm, taps_ref, small_sems.at[0]),
        pltpu.make_async_copy(ids_hbm, ids_ref, small_sems.at[1]),
        pltpu.make_async_copy(dft_hbm, dft_ref, dft_sem),
    ]
    for copy in copies:
        copy.start()
    loads = [
        pltpu.make_async_copy(
            rec_hbm.at[:, pl.ds(width * b, width), :], rec_ref.at[b], rec_sems.at[b]
        )
        for b in range(blocks)
    ]
    for load in loads:
        load.start()
    fir[...] = jnp.zeros(fir.shape, fir.dtype)
    rows = lax.broadcasted_iota(jnp.int32, (2 * LANES, 2 * LANES), 0) % LANES
    cols = lax.broadcasted_iota(jnp.int32, (2 * LANES, 2 * LANES), 1)
    near = (jnp.abs(rows - cols) <= 2) | (cols >= LANES)
    gather = jnp.where(near, 1.0, 0.0).astype(jnp.bfloat16)
    copies[0].wait()
    three = fir_blocks(taps_ref, pad).astype(jnp.bfloat16)
    tiles = samples // LANES
    for i in range(tiles):
        for j in range(max(i - 1, 0), min(i + 2, tiles)):
            fir[LANES * i : LANES * (i + 1), LANES * j : LANES * (j + 1)] = three[
                :, LANES * (j - i + 1) : LANES * (j - i + 2)
            ]
    copies[1].wait()
    copies[2].wait()
    for b in range(blocks):
        loads[b].wait()
        block = rec_ref[b].reshape(windows * width, samples)
        filtered = jnp.dot(block, fir[...], preferred_element_type=jnp.float32).astype(jnp.bfloat16)
        spectra = jnp.dot(filtered, dft_ref[...], preferred_element_type=jnp.float32)
        re, im = spectra[:, :LANES], spectra[:, LANES:]
        amp = jnp.sqrt(re * re + im * im)
        high = amp.astype(jnp.bfloat16)
        low = (amp - high.astype(jnp.float32)).astype(jnp.bfloat16)
        both = jnp.dot(
            jnp.concatenate([high, low], axis=1), gather, preferred_element_type=jnp.float32
        )
        smooth = both[:, :LANES] * (1.0 / 5.0)
        mean_amp = both[:, LANES:] * (1.0 / BINS) + 1e-06
        scale = 1.0 / jnp.maximum(smooth, 0.5 * mean_amp)
        for which, value in enumerate((re, im)):
            unit = (value * scale).astype(jnp.bfloat16)
            white[which, b] = unit.reshape(windows, width, LANES)
            sums[which, b] = jnp.sum(
                unit.astype(jnp.float32).reshape(windows, width, LANES), axis=1
            )
    for k in range(blocks):
        b = relative(me_ref[0], k, blocks)
        re, im = [], []
        for s in range(count):
            total_re = jnp.zeros((width, LANES), jnp.float32)
            total_im = jnp.zeros((width, LANES), jnp.float32)
            for w in range(windows):
                src_re = sums[0, ids_ref[s], w : w + 1, :]
                src_im = sums[1, ids_ref[s], w : w + 1, :]
                white_re = white[0, b, w].astype(jnp.float32)
                white_im = white[1, b, w].astype(jnp.float32)
                total_re += white_re * src_re + white_im * src_im
                total_im += white_im * src_re - white_re * src_im
            re.append(total_re)
            im.append(total_im)
        out_ref[width * k : width * (k + 1), :] = pack(re, im).astype(jnp.bfloat16)


def relative(me, k, size):
    if size & (size - 1) == 0:
        return me ^ k
    return (me + k) % size


def local_cross(me, source_ids, records, taps, dft):
    windows, channels, samples = records.shape
    blocks = channels // BLOCK
    hbm = pl.BlockSpec(memory_space=pltpu.HBM)
    return pl.pallas_call(
        spectra_kernel,
        out_shape=jax.ShapeDtypeStruct((channels, 6 * LANES), jnp.bfloat16),
        in_specs=[pl.BlockSpec(memory_space=pltpu.SMEM), hbm, hbm, hbm, hbm],
        out_specs=pl.BlockSpec(memory_space=pltpu.VMEM),
        scratch_shapes=[
            pltpu.SMEM(source_ids.shape, jnp.int32),
            pltpu.VMEM((blocks, windows, BLOCK, samples), jnp.bfloat16),
            pltpu.VMEM(taps.shape, jnp.float32),
            pltpu.VMEM(dft.shape, jnp.bfloat16),
            pltpu.VMEM((8, LANES), jnp.float32),
            pltpu.VMEM((samples, samples), jnp.bfloat16),
            pltpu.VMEM((2, blocks, windows, BLOCK, LANES), jnp.bfloat16),
            pltpu.VMEM((2, blocks, windows, LANES), jnp.float32),
            pltpu.SemaphoreType.DMA((2,)),
            pltpu.SemaphoreType.DMA,
            pltpu.SemaphoreType.DMA((blocks,)),
        ],
        compiler_params=pltpu.CompilerParams(vmem_limit_bytes=VMEM_LIMIT),
    )(me, *(pltpu.with_memory_space_constraint(v, pltpu.HBM) for v in (source_ids, records, taps, dft)))


def add_kernel(pieces, *refs):
    inputs, outputs = refs[: len(refs) - pieces], refs[len(refs) - pieces :]
    rows = outputs[0].shape[0]
    for k, out in enumerate(outputs):
        at = slice(rows * k, rows * (k + 1))
        total = inputs[0][at, :].astype(jnp.float32)
        for ref in inputs[1:]:
            total += ref[at, :].astype(jnp.float32)
        out[...] = total.astype(out.dtype)


def added(arrays, pieces):
    rows, width = arrays[0].shape
    vmem = pl.BlockSpec(memory_space=pltpu.VMEM)
    return pl.pallas_call(
        functools.partial(add_kernel, pieces),
        out_shape=[jax.ShapeDtypeStruct((rows // pieces, width), jnp.bfloat16)] * pieces,
        in_specs=[vmem] * len(arrays),
        out_specs=[vmem] * pieces,
        compiler_params=pltpu.CompilerParams(vmem_limit_bytes=VMEM_LIMIT),
    )(*arrays)


def gather_kernel(core_ref, *refs):
    own, first, rest, out = refs[0], refs[1], refs[2:-1], refs[-1]
    total = jnp.where(core_ref[0] == 0, own[...].astype(jnp.float32), first[...].astype(jnp.float32))
    for ref in rest:
        total += ref[...].astype(jnp.float32)
    out[...] = total.astype(out.dtype)


def gathered(core, arrays):
    vmem = pl.BlockSpec(memory_space=pltpu.VMEM)
    smem = pl.BlockSpec(memory_space=pltpu.SMEM)
    return pl.pallas_call(
        gather_kernel,
        out_shape=jax.ShapeDtypeStruct(arrays[0].shape, jnp.bfloat16),
        in_specs=[smem] + [vmem] * len(arrays),
        out_specs=vmem,
        compiler_params=pltpu.CompilerParams(vmem_limit_bytes=VMEM_LIMIT),
    )(core, *arrays)


def lag_kernel(scale, table_ref, *refs):
    out = refs[-1]
    total = refs[0][...].astype(jnp.float32)
    for ref in refs[1:-1]:
        total += ref[...].astype(jnp.float32)
    cross = unpack(total)
    high = cross.astype(jnp.bfloat16)
    low = (cross - high.astype(jnp.float32)).astype(jnp.bfloat16)
    dot = functools.partial(jnp.dot, preferred_element_type=jnp.float32)
    top, bottom = table_ref[: 2 * LANES, :], table_ref[2 * LANES :, :]
    lags = dot(high, top) + (dot(low, top) + dot(high, bottom))
    out[...] = (scale * lags).reshape(out.shape)


def to_lags(scale, table, arrays):
    vmem = pl.BlockSpec(memory_space=pltpu.VMEM)
    return pl.pallas_call(
        functools.partial(lag_kernel, scale),
        out_shape=jax.ShapeDtypeStruct((4, BLOCK, LAGS), jnp.float32),
        in_specs=[vmem] * (1 + len(arrays)),
        out_specs=vmem,
        compiler_params=pltpu.CompilerParams(vmem_limit_bytes=VMEM_LIMIT),
    )(table, *arrays)


def from_peers(value, axis):
    size = lax.axis_size(axis)
    return [
        lax.ppermute(value, axis, [(i, (i + k) % size) for i in range(size)])
        for k in range(1, size)
    ]


def body(records, fir_taps, source_ids):
    samples = records.shape[2]
    chans, times, cores = (lax.axis_size(axis) for axis in ("chan", "tm", "rep"))
    me = lax.axis_index("chan").astype(jnp.int32).reshape(1)
    core = lax.axis_index("rep").astype(jnp.int32).reshape(1)
    cross = local_cross(me, source_ids, records, fir_taps.reshape(1, -1), jnp.asarray(dft_table(samples)))
    pieces = added([cross] + from_peers(cross, "rep"), chans)
    mesh = [(a, t, r) for a in range(chans) for t in range(times) for r in range(cores)]
    place = {where: index for index, where in enumerate(mesh)}
    arrived = []
    for turn in range(-(-times // cores)):
        for k in range(chans):
            pairs = []
            for a, t, r in mesh:
                ahead = turn * cores + r
                if ahead >= times or (ahead == 0 and k == 0):
                    continue
                pairs.append((place[a, t, r], place[relative(a, k, chans), (t + ahead) % times, r]))
            arrived.append(lax.ppermute(pieces[k], ("chan", "tm", "rep"), pairs))
    total = gathered(core, [pieces[0]] + arrived)
    windows_all = records.shape[0] * chans * times * cores
    scale = 1.0 / math.sqrt(windows_all * BLOCK * BINS)
    return to_lags(scale, jnp.asarray(lag_table(samples)), [total] + from_peers(total, "rep"))


def solution(mesh):
    in_specs = (P(("chan", "tm", "rep"), "parts", None), P(), P("parts"))
    out_specs = P(None, ("parts", "chan"), None)
    return jax.shard_map(body, mesh=mesh, in_specs=in_specs, out_specs=out_specs, check_vma=False)
```

```python
import functools
import math

import jax
import jax.numpy as jnp
import numpy as np
from jax import lax
from jax.experimental import pallas as pl
from jax.experimental.pallas import tpu as pltpu
from jax.sharding import PartitionSpec as P

BINS = 96
LAGS = 256
BLOCK = 64
LANES = 128
VMEM_LIMIT = 32 * 1024 * 1024


def dft_table(samples):
    times = np.arange(samples)[:, None]
    freqs = np.arange(1, BINS + 1)[None, :]
    angle = np.float32(2.0 * math.pi / samples) * (times * freqs % samples).astype(np.float32)
    table = np.zeros((samples, 2 * LANES), np.float32)
    table[:, :BINS] = np.cos(angle)
    table[:, LANES : LANES + BINS] = -np.sin(angle)
    return table.astype(jnp.bfloat16)


def lag_table(samples):
    freqs = np.arange(1, BINS + 1)[:, None]
    shifts = np.arange(LAGS)[None, :] - LAGS // 2
    angle = np.float32(2.0 * math.pi / samples) * np.mod(freqs * shifts, samples).astype(np.float32)
    table = np.zeros((2 * LANES, LAGS), np.float32)
    table[:BINS] = np.cos(angle)
    table[LANES : LANES + BINS] = -np.sin(angle)
    high = table.astype(jnp.bfloat16)
    low = (table - high.astype(np.float32)).astype(jnp.bfloat16)
    return np.concatenate([high, low], axis=0)


def fir_blocks(taps_ref, pad_ref):
    taps = taps_ref.shape[1]
    half = taps // 2
    pad_ref[...] = jnp.zeros(pad_ref.shape, jnp.float32)
    pad_ref[0:1, 0:taps] = taps_ref[...]
    rows = lax.broadcasted_iota(jnp.int32, (LANES, LANES), 0)
    cols = lax.broadcasted_iota(jnp.int32, (LANES, LANES), 1)
    flip = (rows + cols == taps - 1).astype(jnp.bfloat16)
    turned = jnp.dot(
        pad_ref[...].astype(jnp.bfloat16), flip, preferred_element_type=jnp.float32
    )[0:1]
    wide = jnp.concatenate([turned, jnp.zeros((1, 2 * LANES), jnp.float32)], axis=1)
    wide = jnp.broadcast_to(wide, (LANES, 3 * LANES))
    return pltpu.roll(wide, LANES - half, 1, stride=1, stride_axis=0)


def pack(re, im):
    lane = lax.broadcasted_iota(jnp.int32, re[0].shape, 1)
    tiles = []
    for index in range(3):
        for part, last in ((re[index], re[3]), (im[index], im[3])):
            moved = pltpu.roll(last, BINS - 32 * index, 1)
            tiles.append(jnp.where(lane < BINS, part, moved))
    return jnp.concatenate(tiles, axis=1)


def unpack(packed):
    lane = lax.broadcasted_iota(jnp.int32, (packed.shape[0], LANES), 1)
    tiles = [packed[:, LANES * i : LANES * (i + 1)] for i in range(6)]
    last = []
    for which in range(2):
        total = jnp.zeros_like(tiles[0])
        for index in range(3):
            moved = pltpu.roll(tiles[2 * index + which], LANES - BINS + 32 * index, 1)
            total = jnp.where((lane >= 32 * index) & (lane < 32 * index + 32), moved, total)
        last.append(total)
    rows = [jnp.concatenate([tiles[2 * i], tiles[2 * i + 1]], axis=1) for i in range(3)]
    return jnp.concatenate(rows + [jnp.concatenate(last, axis=1)], axis=0)


def spectra_kernel(
    place_ref,
    ids_hbm,
    rec_hbm,
    taps_hbm,
    dft_hbm,
    out_ref,
    kept_ref,
    ids_ref,
    rec_ref,
    taps_ref,
    dft_ref,
    pad,
    fir,
    white,
    sums,
    small_sems,
    dft_sem,
    rec_sems,
):
    blocks, windows, width, samples = rec_ref.shape
    count = ids_ref.shape[0]
    copies = [
        pltpu.make_async_copy(taps_hbm, taps_ref, small_sems.at[0]),
        pltpu.make_async_copy(ids_hbm, ids_ref, small_sems.at[1]),
        pltpu.make_async_copy(dft_hbm, dft_ref, dft_sem),
    ]
    for copy in copies:
        copy.start()
    loads = [
        pltpu.make_async_copy(
            rec_hbm.at[:, pl.ds(width * b, width), :], rec_ref.at[b], rec_sems.at[b]
        )
        for b in range(blocks)
    ]
    for load in loads:
        load.start()
    fir[...] = jnp.zeros(fir.shape, fir.dtype)
    rows = lax.broadcasted_iota(jnp.int32, (2 * LANES, 2 * LANES), 0) % LANES
    cols = lax.broadcasted_iota(jnp.int32, (2 * LANES, 2 * LANES), 1)
    near = (jnp.abs(rows - cols) <= 2) | (cols >= LANES)
    gather = jnp.where(near, 1.0, 0.0).astype(jnp.bfloat16)
    copies[0].wait()
    three = fir_blocks(taps_ref, pad).astype(jnp.bfloat16)
    tiles = samples // LANES
    for i in range(tiles):
        for j in range(max(i - 1, 0), min(i + 2, tiles)):
            fir[LANES * i : LANES * (i + 1), LANES * j : LANES * (j + 1)] = three[
                :, LANES * (j - i + 1) : LANES * (j - i + 2)
            ]
    copies[2].wait()
    both_tables = jnp.dot(fir[...], dft_ref[...], preferred_element_type=jnp.float32).astype(
        jnp.bfloat16
    )
    copies[1].wait()
    for load in loads:
        load.wait()
    spectra, both = [], []
    for b in range(blocks):
        block = rec_ref[b].reshape(windows * width, samples)
        spectra.append(jnp.dot(block, both_tables, preferred_element_type=jnp.float32))
    for b in range(blocks):
        re, im = spectra[b][:, :LANES], spectra[b][:, LANES:]
        amp = jnp.sqrt(re * re + im * im)
        high = amp.astype(jnp.bfloat16)
        low = (amp - high.astype(jnp.float32)).astype(jnp.bfloat16)
        both.append(
            jnp.dot(
                jnp.concatenate([high, low], axis=1), gather, preferred_element_type=jnp.float32
            )
        )
    for b in range(blocks):
        smooth = both[b][:, :LANES] * (1.0 / 5.0)
        mean_amp = both[b][:, LANES:] * (1.0 / BINS) + 1e-06
        scale = 1.0 / jnp.maximum(smooth, 0.5 * mean_amp)
        for which in range(2):
            value = spectra[b][:, LANES * which : LANES * (which + 1)]
            unit = (value * scale).astype(jnp.bfloat16)
            white[which, b] = unit.reshape(windows, width, LANES)
            sums[which, b] = jnp.sum(
                unit.astype(jnp.float32).reshape(windows, width, LANES), axis=1
            )

    def cross(k, rows):
        b = relative(place_ref[0], k, blocks)
        re, im = [], []
        for s in range(count):
            total_re = jnp.zeros((rows.size, LANES), jnp.float32)
            total_im = jnp.zeros((rows.size, LANES), jnp.float32)
            for w in range(windows):
                src_re = sums[0, ids_ref[s], w : w + 1, :]
                src_im = sums[1, ids_ref[s], w : w + 1, :]
                white_re = white[0, b, w, rows, :].astype(jnp.float32)
                white_im = white[1, b, w, rows, :].astype(jnp.float32)
                total_re += white_re * src_re + white_im * src_im
                total_im += white_im * src_re - white_re * src_im
            re.append(total_re)
            im.append(total_im)
        return pack(re, im).astype(jnp.bfloat16)

    whole, shared = kinds(blocks)
    half = width // 2
    mine = pl.ds(pl.multiple_of(place_ref[1] * half, half), half)
    theirs = pl.ds(pl.multiple_of((1 - place_ref[1]) * half, half), half)
    for i, k in enumerate(whole):
        out_ref[width * i : width * (i + 1), :] = cross(k, pl.ds(0, width))
    for i, k in enumerate(shared):
        start = width * len(whole) + half * i
        out_ref[start : start + half, :] = cross(k, theirs)
        kept_ref[half * i : half * (i + 1), :] = cross(k, mine)


def kinds(blocks):
    return list(range(3 * blocks // 4 - 1, 0, -1)), list(range(3 * blocks // 4, blocks)) + [0]


def relative(me, k, size):
    if size & (size - 1) == 0:
        return me ^ k
    return (me + k) % size


def local_cross(place, source_ids, records, taps, dft):
    windows, channels, samples = records.shape
    blocks = channels // BLOCK
    whole, shared = (len(kind) for kind in kinds(blocks))
    half = BLOCK // 2
    hbm = pl.BlockSpec(memory_space=pltpu.HBM)
    return pl.pallas_call(
        spectra_kernel,
        out_shape=[
            jax.ShapeDtypeStruct((BLOCK * whole + half * shared, 6 * LANES), jnp.bfloat16),
            jax.ShapeDtypeStruct((half * shared, 6 * LANES), jnp.bfloat16),
        ],
        in_specs=[pl.BlockSpec(memory_space=pltpu.SMEM), hbm, hbm, hbm, hbm],
        out_specs=[pl.BlockSpec(memory_space=pltpu.VMEM)] * 2,
        scratch_shapes=[
            pltpu.SMEM(source_ids.shape, jnp.int32),
            pltpu.VMEM((blocks, windows, BLOCK, samples), jnp.bfloat16),
            pltpu.VMEM(taps.shape, jnp.float32),
            pltpu.VMEM(dft.shape, jnp.bfloat16),
            pltpu.VMEM((8, LANES), jnp.float32),
            pltpu.VMEM((samples, samples), jnp.bfloat16),
            pltpu.VMEM((2, blocks, windows, BLOCK, LANES), jnp.bfloat16),
            pltpu.VMEM((2, blocks, windows, LANES), jnp.float32),
            pltpu.SemaphoreType.DMA((2,)),
            pltpu.SemaphoreType.DMA,
            pltpu.SemaphoreType.DMA((blocks,)),
        ],
        compiler_params=pltpu.CompilerParams(vmem_limit_bytes=VMEM_LIMIT),
    )(place, *(pltpu.with_memory_space_constraint(v, pltpu.HBM) for v in (source_ids, records, taps, dft)))


def tree(values):
    while len(values) > 1:
        values = [sum(values[i + 1 : i + 2], values[i]) for i in range(0, len(values), 2)]
    return values[0]


def add_kernel(whole, own, kept, other, *outs):
    rows = outs[0].shape[0]
    for i, out in enumerate(outs):
        if i < whole:
            at = slice(rows * i, rows * (i + 1))
            mine = own[at, :]
        else:
            half = out.shape[0]
            mine = kept[half * (i - whole) : half * (i - whole + 1), :]
            start = rows * whole + half * (i - whole)
            at = slice(start, start + half)
        total = mine.astype(jnp.float32) + other[at, :].astype(jnp.float32)
        out[...] = total.astype(out.dtype)


def tree_kernel(*refs):
    refs[-1][...] = tree([ref[...].astype(jnp.float32) for ref in refs[:-1]]).astype(refs[-1].dtype)


def core_kernel(turns, shares, *refs):
    out = refs[-1]
    arrived = [ref[...].astype(jnp.float32) for ref in refs[:-1]]
    share, arrived = tree(arrived[:shares]), arrived[shares:]
    blocks = [tree(arrived[i : i + turns]) for i in range(0, len(arrived), turns)]
    total = functools.reduce(jnp.add, blocks)
    rows = total.shape[0]
    out[:rows, :] = total.astype(out.dtype)
    out[rows:, :] = share.astype(out.dtype)


def lag_kernel(scale, place_ref, table_ref, own, other, out, total):
    rows = total.shape[0]
    half = rows // 2
    total[...] = own[:rows, :].astype(jnp.float32) + other[:rows, :].astype(jnp.float32)
    for core, ref in ((place_ref[1], own), (1 - place_ref[1], other)):
        at = pl.ds(pl.multiple_of(core * half, half), half)
        total[at, :] += ref[rows:, :].astype(jnp.float32)
    cross = unpack(total[...])
    high = cross.astype(jnp.bfloat16)
    low = (cross - high.astype(jnp.float32)).astype(jnp.bfloat16)
    dot = functools.partial(jnp.dot, preferred_element_type=jnp.float32)
    top, bottom = table_ref[: 2 * LANES, :], table_ref[2 * LANES :, :]
    lags = dot(high, top) + (dot(low, top) + dot(high, bottom))
    out[...] = (scale * lags).reshape(out.shape)


def in_vmem(kernel, out_shape, inputs, scalars=0, scratch=()):
    vmem = pl.BlockSpec(memory_space=pltpu.VMEM)
    smem = pl.BlockSpec(memory_space=pltpu.SMEM)
    several = isinstance(out_shape, list)
    return pl.pallas_call(
        kernel,
        out_shape=out_shape,
        in_specs=[smem] * scalars + [vmem] * (len(inputs) - scalars),
        out_specs=[vmem] * len(out_shape) if several else vmem,
        scratch_shapes=scratch,
        compiler_params=pltpu.CompilerParams(vmem_limit_bytes=VMEM_LIMIT),
    )(*inputs)


def body(records, fir_taps, source_ids):
    samples = records.shape[2]
    chans, times, cores = (lax.axis_size(axis) for axis in ("chan", "tm", "rep"))
    assert cores == 2
    axes = ("chan", "tm", "rep")
    devices = [(a, t, r) for a in range(chans) for t in range(times) for r in range(cores)]
    number = {device: i for i, device in enumerate(devices)}

    def send(value, to):
        return lax.ppermute(value, axes, [(number[d], number[to(*d)]) for d in devices])

    place = jnp.stack([lax.axis_index("chan"), lax.axis_index("rep")]).astype(jnp.int32)
    own, kept = local_cross(
        place, source_ids, records, fir_taps.reshape(1, -1), jnp.asarray(dft_table(samples))
    )
    width, half = 6 * LANES, BLOCK // 2
    whole, shared = kinds(chans)
    other = send(own, lambda a, t, r: (a, t, 1 - r))
    full = jax.ShapeDtypeStruct((BLOCK, width), jnp.bfloat16)
    part = jax.ShapeDtypeStruct((half, width), jnp.bfloat16)
    pieces = in_vmem(
        functools.partial(add_kernel, len(whole)),
        [full] * len(whole) + [part] * len(shared),
        [own, kept, other],
    )
    shares = [
        send(piece, lambda a, t, r, k=k: (relative(a, k, chans), t, r))
        for k, piece in zip(shared[:-1], pieces[len(whole) :])
    ]
    arrived = [
        send(piece, lambda a, t, r, k=k: (relative(a, k, chans), relative(t, turn + r, times), r))
        for k, piece in zip(whole, pieces)
        for turn in range(0, times, cores)
    ]
    share = in_vmem(tree_kernel, part, [pieces[-1]] + shares)
    shares = [share] + [
        send(share, lambda a, t, r, j=j: (a, relative(t, j, times), r)) for j in range(1, times)
    ]
    total = in_vmem(
        functools.partial(core_kernel, -(-times // cores), times),
        jax.ShapeDtypeStruct((BLOCK + half, width), jnp.bfloat16),
        shares + arrived,
    )
    other = send(total, lambda a, t, r: (a, t, 1 - r))
    windows_all = records.shape[0] * chans * times * cores
    scale = 1.0 / math.sqrt(windows_all * BLOCK * BINS)
    return in_vmem(
        functools.partial(lag_kernel, scale),
        jax.ShapeDtypeStruct((source_ids.shape[0], BLOCK, LAGS), jnp.float32),
        [place, jnp.asarray(lag_table(samples)), total, other],
        scalars=1,
        scratch=[pltpu.VMEM((BLOCK, width), jnp.float32)],
    )


def solution(mesh):
    in_specs = (P(("chan", "tm", "rep"), "parts", None), P(), P("parts"))
    out_specs = P(None, ("parts", "chan"), None)
    return jax.shard_map(body, mesh=mesh, in_specs=in_specs, out_specs=out_specs, check_vma=False)
```

```python
import functools
import math

import jax
import jax.numpy as jnp
import numpy as np
from jax import lax
from jax.experimental import pallas as pl
from jax.experimental.pallas import tpu as pltpu
from jax.sharding import PartitionSpec as P

BINS = 96
LAGS = 256
BLOCK = 64
LANES = 128
VMEM_LIMIT = 32 * 1024 * 1024


def dft_table(samples):
    times = np.arange(samples)[:, None]
    freqs = np.arange(1, BINS + 1)[None, :]
    angle = np.float32(2.0 * math.pi / samples) * (times * freqs % samples).astype(np.float32)
    table = np.zeros((samples, 2 * LANES), np.float32)
    table[:, :BINS] = np.cos(angle)
    table[:, LANES : LANES + BINS] = -np.sin(angle)
    return table.astype(jnp.bfloat16)


def lag_table(samples):
    freqs = np.arange(1, BINS + 1)[:, None]
    shifts = np.arange(LAGS)[None, :] - LAGS // 2
    angle = np.float32(2.0 * math.pi / samples) * np.mod(freqs * shifts, samples).astype(np.float32)
    table = np.zeros((2 * LANES, LAGS), np.float32)
    table[:BINS] = np.cos(angle)
    table[LANES : LANES + BINS] = -np.sin(angle)
    high = table.astype(jnp.bfloat16)
    low = (table - high.astype(np.float32)).astype(jnp.bfloat16)
    return np.concatenate([high, low], axis=0)


def fir_blocks(taps_ref, pad_ref):
    taps = taps_ref.shape[1]
    half = taps // 2
    pad_ref[...] = jnp.zeros(pad_ref.shape, jnp.float32)
    pad_ref[0:1, 0:taps] = taps_ref[...]
    rows = lax.broadcasted_iota(jnp.int32, (LANES, LANES), 0)
    cols = lax.broadcasted_iota(jnp.int32, (LANES, LANES), 1)
    flip = (rows + cols == taps - 1).astype(jnp.bfloat16)
    turned = jnp.dot(
        pad_ref[...].astype(jnp.bfloat16), flip, preferred_element_type=jnp.float32
    )[0:1]
    wide = jnp.concatenate([turned, jnp.zeros((1, 2 * LANES), jnp.float32)], axis=1)
    wide = jnp.broadcast_to(wide, (LANES, 3 * LANES))
    return pltpu.roll(wide, LANES - half, 1, stride=1, stride_axis=0)


def pack(re, im):
    lane = lax.broadcasted_iota(jnp.int32, re[0].shape, 1)
    tiles = []
    for index in range(3):
        for part, last in ((re[index], re[3]), (im[index], im[3])):
            moved = pltpu.roll(last, BINS - 32 * index, 1)
            tiles.append(jnp.where(lane < BINS, part, moved))
    return jnp.concatenate(tiles, axis=1)


def unpack(packed):
    lane = lax.broadcasted_iota(jnp.int32, (packed.shape[0], LANES), 1)
    tiles = [packed[:, LANES * i : LANES * (i + 1)] for i in range(6)]
    last = []
    for which in range(2):
        total = jnp.zeros_like(tiles[0])
        for index in range(3):
            moved = pltpu.roll(tiles[2 * index + which], LANES - BINS + 32 * index, 1)
            total = jnp.where((lane >= 32 * index) & (lane < 32 * index + 32), moved, total)
        last.append(total)
    rows = [jnp.concatenate([tiles[2 * i], tiles[2 * i + 1]], axis=1) for i in range(3)]
    return jnp.concatenate(rows + [jnp.concatenate(last, axis=1)], axis=0)


def spectra_kernel(
    ids_hbm,
    rec_hbm,
    taps_hbm,
    dft_hbm,
    out_ref,
    kept_ref,
    ids_ref,
    rec_ref,
    taps_ref,
    dft_ref,
    pad,
    fir,
    white,
    sums,
    small_sems,
    dft_sem,
    rec_sems,
):
    blocks, windows, width, samples = rec_ref.shape
    count = ids_ref.shape[0]
    copies = [
        pltpu.make_async_copy(taps_hbm, taps_ref, small_sems.at[0]),
        pltpu.make_async_copy(ids_hbm, ids_ref, small_sems.at[1]),
        pltpu.make_async_copy(dft_hbm, dft_ref, dft_sem),
    ]
    for copy in copies:
        copy.start()
    loads = [
        pltpu.make_async_copy(
            rec_hbm.at[:, pl.ds(width * b, width), :], rec_ref.at[b], rec_sems.at[b]
        )
        for b in range(blocks)
    ]
    for load in loads:
        load.start()
    fir[...] = jnp.zeros(fir.shape, fir.dtype)
    rows = lax.broadcasted_iota(jnp.int32, (2 * LANES, 2 * LANES), 0) % LANES
    cols = lax.broadcasted_iota(jnp.int32, (2 * LANES, 2 * LANES), 1)
    near = (jnp.abs(rows - cols) <= 2) | (cols >= LANES)
    gather = jnp.where(near, 1.0, 0.0).astype(jnp.bfloat16)
    copies[0].wait()
    three = fir_blocks(taps_ref, pad).astype(jnp.bfloat16)
    tiles = samples // LANES
    for i in range(tiles):
        for j in range(max(i - 1, 0), min(i + 2, tiles)):
            fir[LANES * i : LANES * (i + 1), LANES * j : LANES * (j + 1)] = three[
                :, LANES * (j - i + 1) : LANES * (j - i + 2)
            ]
    copies[2].wait()
    both_tables = jnp.dot(fir[...], dft_ref[...], preferred_element_type=jnp.float32).astype(
        jnp.bfloat16
    )
    copies[1].wait()
    for load in loads:
        load.wait()
    spectra, both = [], []
    for b in range(blocks):
        block = rec_ref[b].reshape(windows * width, samples)
        spectra.append(jnp.dot(block, both_tables, preferred_element_type=jnp.float32))
    for b in range(blocks):
        re, im = spectra[b][:, :LANES], spectra[b][:, LANES:]
        amp = jnp.sqrt(re * re + im * im)
        high = amp.astype(jnp.bfloat16)
        low = (amp - high.astype(jnp.float32)).astype(jnp.bfloat16)
        both.append(
            jnp.dot(
                jnp.concatenate([high, low], axis=1), gather, preferred_element_type=jnp.float32
            )
        )
    for b in range(blocks):
        smooth = both[b][:, :LANES] * (1.0 / 5.0)
        mean_amp = both[b][:, LANES:] * (1.0 / BINS) + 1e-06
        scale = 1.0 / jnp.maximum(smooth, 0.5 * mean_amp)
        for which in range(2):
            value = spectra[b][:, LANES * which : LANES * (which + 1)]
            unit = (value * scale).astype(jnp.bfloat16)
            white[which, b] = unit.reshape(windows, width, LANES)
            sums[which, b] = jnp.sum(
                unit.astype(jnp.float32).reshape(windows, width, LANES), axis=1
            )

    def cross(k):
        b = relative(lax.axis_index("chan"), k, blocks)
        re, im = [], []
        for s in range(count):
            total_re = jnp.zeros((width, LANES), jnp.float32)
            total_im = jnp.zeros((width, LANES), jnp.float32)
            for w in range(windows):
                src_re = sums[0, ids_ref[s], w : w + 1, :]
                src_im = sums[1, ids_ref[s], w : w + 1, :]
                white_re = white[0, b, w].astype(jnp.float32)
                white_im = white[1, b, w].astype(jnp.float32)
                total_re += white_re * src_re + white_im * src_im
                total_im += white_im * src_re - white_re * src_im
            re.append(total_re)
            im.append(total_im)
        return pack(re, im).astype(jnp.bfloat16)

    whole, shared = kinds(blocks)
    half = width // 2
    first = lax.axis_index("rep") == 0
    for i, k in enumerate(whole):
        out_ref[width * i : width * (i + 1), :] = cross(k)
    for i, k in enumerate(shared):
        start = width * len(whole) + half * i
        value = cross(k)
        top, bottom = value[:half], value[half:]
        out_ref[start : start + half, :] = jnp.where(first, bottom, top)
        kept_ref[half * i : half * (i + 1), :] = jnp.where(first, top, bottom)


def kinds(blocks):
    return list(range(3 * blocks // 4 - 1, 0, -1)), list(range(3 * blocks // 4, blocks)) + [0]


def relative(me, k, size):
    if size & (size - 1) == 0:
        return me ^ k
    return (me + k) % size


def local_cross(source_ids, records, taps, dft):
    windows, channels, samples = records.shape
    blocks = channels // BLOCK
    whole, shared = (len(kind) for kind in kinds(blocks))
    half = BLOCK // 2
    hbm = pl.BlockSpec(memory_space=pltpu.HBM)
    return pl.pallas_call(
        spectra_kernel,
        out_shape=[
            jax.ShapeDtypeStruct((BLOCK * whole + half * shared, 6 * LANES), jnp.bfloat16),
            jax.ShapeDtypeStruct((half * shared, 6 * LANES), jnp.bfloat16),
        ],
        in_specs=[hbm] * 4,
        out_specs=[pl.BlockSpec(memory_space=pltpu.VMEM)] * 2,
        scratch_shapes=[
            pltpu.SMEM(source_ids.shape, jnp.int32),
            pltpu.VMEM((blocks, windows, BLOCK, samples), jnp.bfloat16),
            pltpu.VMEM(taps.shape, jnp.float32),
            pltpu.VMEM(dft.shape, jnp.bfloat16),
            pltpu.VMEM((8, LANES), jnp.float32),
            pltpu.VMEM((samples, samples), jnp.bfloat16),
            pltpu.VMEM((2, blocks, windows, BLOCK, LANES), jnp.bfloat16),
            pltpu.VMEM((2, blocks, windows, LANES), jnp.float32),
            pltpu.SemaphoreType.DMA((2,)),
            pltpu.SemaphoreType.DMA,
            pltpu.SemaphoreType.DMA((blocks,)),
        ],
        compiler_params=pltpu.CompilerParams(vmem_limit_bytes=VMEM_LIMIT),
    )(*(pltpu.with_memory_space_constraint(v, pltpu.HBM) for v in (source_ids, records, taps, dft)))


def tree(values):
    while len(values) > 1:
        values = [sum(values[i + 1 : i + 2], values[i]) for i in range(0, len(values), 2)]
    return values[0]


def add_kernel(whole, own, kept, other, *outs):
    rows = outs[0].shape[0]
    for i, out in enumerate(outs):
        if i < whole:
            at = slice(rows * i, rows * (i + 1))
            mine = own[at, :]
        else:
            half = out.shape[0]
            mine = kept[half * (i - whole) : half * (i - whole + 1), :]
            start = rows * whole + half * (i - whole)
            at = slice(start, start + half)
        total = mine.astype(jnp.float32) + other[at, :].astype(jnp.float32)
        out[...] = total.astype(out.dtype)


def tree_kernel(*refs):
    refs[-1][...] = tree([ref[...].astype(jnp.float32) for ref in refs[:-1]]).astype(refs[-1].dtype)


def core_kernel(turns, shares, *refs):
    out = refs[-1]
    arrived = [ref[...].astype(jnp.float32) for ref in refs[:-1]]
    share, arrived = tree(arrived[:shares]), arrived[shares:]
    blocks = [tree(arrived[i : i + turns]) for i in range(0, len(arrived), turns)]
    total = functools.reduce(jnp.add, blocks)
    rows = total.shape[0]
    out[:rows, :] = total.astype(out.dtype)
    out[rows:, :] = share.astype(out.dtype)


def lag_kernel(scale, table_ref, own, other, out):
    rows = out.shape[1]
    first = lax.axis_index("rep") == 0
    mine, theirs = own[rows:, :].astype(jnp.float32), other[rows:, :].astype(jnp.float32)
    shares = jnp.concatenate(
        [jnp.where(first, mine, theirs), jnp.where(first, theirs, mine)], axis=0
    )
    total = own[:rows, :].astype(jnp.float32) + other[:rows, :].astype(jnp.float32) + shares
    cross = unpack(total)
    high = cross.astype(jnp.bfloat16)
    low = (cross - high.astype(jnp.float32)).astype(jnp.bfloat16)
    dot = functools.partial(jnp.dot, preferred_element_type=jnp.float32)
    top, bottom = table_ref[: 2 * LANES, :], table_ref[2 * LANES :, :]
    lags = dot(high, top) + (dot(low, top) + dot(high, bottom))
    out[...] = (scale * lags).reshape(out.shape)


def in_vmem(kernel, out_shape, inputs):
    vmem = pl.BlockSpec(memory_space=pltpu.VMEM)
    several = isinstance(out_shape, list)
    return pl.pallas_call(
        kernel,
        out_shape=out_shape,
        in_specs=[vmem] * len(inputs),
        out_specs=[vmem] * len(out_shape) if several else vmem,
        compiler_params=pltpu.CompilerParams(vmem_limit_bytes=VMEM_LIMIT),
    )(*inputs)


def body(records, fir_taps, source_ids):
    samples = records.shape[2]
    chans, times, cores = (lax.axis_size(axis) for axis in ("chan", "tm", "rep"))
    assert cores == 2
    axes = ("chan", "tm", "rep")
    devices = [(a, t, r) for a in range(chans) for t in range(times) for r in range(cores)]
    number = {device: i for i, device in enumerate(devices)}

    def send(value, to):
        return lax.ppermute(value, axes, [(number[d], number[to(*d)]) for d in devices])

    own, kept = local_cross(
        source_ids, records, fir_taps.reshape(1, -1), jnp.asarray(dft_table(samples))
    )
    width, half = 6 * LANES, BLOCK // 2
    whole, shared = kinds(chans)
    other = send(own, lambda a, t, r: (a, t, 1 - r))
    full = jax.ShapeDtypeStruct((BLOCK, width), jnp.bfloat16)
    part = jax.ShapeDtypeStruct((half, width), jnp.bfloat16)
    pieces = in_vmem(
        functools.partial(add_kernel, len(whole)),
        [full] * len(whole) + [part] * len(shared),
        [own, kept, other],
    )
    shares = [
        send(piece, lambda a, t, r, k=k: (relative(a, k, chans), t, r))
        for k, piece in zip(shared[:-1], pieces[len(whole) :])
    ]
    arrived = [
        send(piece, lambda a, t, r, k=k: (relative(a, k, chans), relative(t, turn + r, times), r))
        for k, piece in zip(whole, pieces)
        for turn in range(0, times, cores)
    ]
    share = in_vmem(tree_kernel, part, [pieces[-1]] + shares)
    shares = [share] + [
        send(share, lambda a, t, r, j=j: (a, relative(t, j, times), r)) for j in range(1, times)
    ]
    total = in_vmem(
        functools.partial(core_kernel, -(-times // cores), times),
        jax.ShapeDtypeStruct((BLOCK + half, width), jnp.bfloat16),
        shares + arrived,
    )
    other = send(total, lambda a, t, r: (a, t, 1 - r))
    windows_all = records.shape[0] * chans * times * cores
    scale = 1.0 / math.sqrt(windows_all * BLOCK * BINS)
    return in_vmem(
        functools.partial(lag_kernel, scale),
        jax.ShapeDtypeStruct((source_ids.shape[0], BLOCK, LAGS), jnp.float32),
        [jnp.asarray(lag_table(samples)), total, other],
    )


def solution(mesh):
    in_specs = (P(("chan", "tm", "rep"), "parts", None), P(), P("parts"))
    out_specs = P(None, ("parts", "chan"), None)
    return jax.shard_map(body, mesh=mesh, in_specs=in_specs, out_specs=out_specs, check_vma=False)
```

```python
import functools
import math

import jax
import jax.numpy as jnp
import numpy as np
from jax import lax
from jax.experimental import pallas as pl
from jax.experimental.pallas import tpu as pltpu
from jax.sharding import PartitionSpec as P

BINS = 96
LAGS = 256
BLOCK = 64
LANES = 128
VMEM_LIMIT = 32 * 1024 * 1024


def dft_table(samples):
    times = np.arange(samples)[:, None]
    freqs = np.arange(1, BINS + 1)[None, :]
    angle = np.float32(2.0 * math.pi / samples) * (times * freqs % samples).astype(np.float32)
    table = np.zeros((samples, 2 * LANES), np.float32)
    table[:, :BINS] = np.cos(angle)
    table[:, LANES : LANES + BINS] = -np.sin(angle)
    return table.astype(jnp.bfloat16)


def lag_table(samples):
    freqs = np.arange(1, BINS + 1)[:, None]
    shifts = np.arange(LAGS)[None, :] - LAGS // 2
    angle = np.float32(2.0 * math.pi / samples) * np.mod(freqs * shifts, samples).astype(np.float32)
    table = np.zeros((2 * LANES, LAGS), np.float32)
    table[:BINS] = np.cos(angle)
    table[LANES : LANES + BINS] = -np.sin(angle)
    high = table.astype(jnp.bfloat16)
    low = (table - high.astype(np.float32)).astype(jnp.bfloat16)
    return np.concatenate([high, low], axis=0)


def fir_blocks(taps_ref, pad_ref):
    taps = taps_ref.shape[1]
    half = taps // 2
    pad_ref[...] = jnp.zeros(pad_ref.shape, jnp.float32)
    pad_ref[0:1, 0:taps] = taps_ref[...]
    rows = lax.broadcasted_iota(jnp.int32, (LANES, LANES), 0)
    cols = lax.broadcasted_iota(jnp.int32, (LANES, LANES), 1)
    flip = (rows + cols == taps - 1).astype(jnp.bfloat16)
    turned = jnp.dot(
        pad_ref[...].astype(jnp.bfloat16), flip, preferred_element_type=jnp.float32
    )[0:1]
    wide = jnp.concatenate([turned, jnp.zeros((1, 2 * LANES), jnp.float32)], axis=1)
    wide = jnp.broadcast_to(wide, (LANES, 3 * LANES))
    return pltpu.roll(wide, LANES - half, 1, stride=1, stride_axis=0)


def pack(re, im):
    lane = lax.broadcasted_iota(jnp.int32, re[0].shape, 1)
    tiles = []
    for index in range(3):
        for part, last in ((re[index], re[3]), (im[index], im[3])):
            moved = pltpu.roll(last, BINS - 32 * index, 1)
            tiles.append(jnp.where(lane < BINS, part, moved))
    return jnp.concatenate(tiles, axis=1)


def unpack(packed):
    lane = lax.broadcasted_iota(jnp.int32, (packed.shape[0], LANES), 1)
    tiles = [packed[:, LANES * i : LANES * (i + 1)] for i in range(6)]
    last = []
    for which in range(2):
        total = jnp.zeros_like(tiles[0])
        for index in range(3):
            moved = pltpu.roll(tiles[2 * index + which], LANES - BINS + 32 * index, 1)
            total = jnp.where((lane >= 32 * index) & (lane < 32 * index + 32), moved, total)
        last.append(total)
    rows = [jnp.concatenate([tiles[2 * i], tiles[2 * i + 1]], axis=1) for i in range(3)]
    return jnp.concatenate(rows + [jnp.concatenate(last, axis=1)], axis=0)


def spectra_kernel(
    ids_hbm,
    rec_hbm,
    taps_hbm,
    dft_hbm,
    out_ref,
    kept_ref,
    ids_ref,
    rec_ref,
    taps_ref,
    dft_ref,
    pad,
    fir,
    white,
    sums,
    small_sems,
    dft_sem,
    rec_sems,
):
    blocks, windows, width, samples = rec_ref.shape
    count = ids_ref.shape[0]
    copies = [
        pltpu.make_async_copy(taps_hbm, taps_ref, small_sems.at[0]),
        pltpu.make_async_copy(ids_hbm, ids_ref, small_sems.at[1]),
        pltpu.make_async_copy(dft_hbm, dft_ref, dft_sem),
    ]
    for copy in copies:
        copy.start()
    loads = [
        pltpu.make_async_copy(
            rec_hbm.at[:, pl.ds(width * b, width), :], rec_ref.at[b], rec_sems.at[b]
        )
        for b in range(blocks)
    ]
    for load in loads:
        load.start()
    fir[...] = jnp.zeros(fir.shape, fir.dtype)
    rows = lax.broadcasted_iota(jnp.int32, (2 * LANES, 2 * LANES), 0) % LANES
    cols = lax.broadcasted_iota(jnp.int32, (2 * LANES, 2 * LANES), 1)
    near = (jnp.abs(rows - cols) <= 2) | (cols >= LANES)
    gather = jnp.where(near, 1.0, 0.0).astype(jnp.bfloat16)
    copies[0].wait()
    three = fir_blocks(taps_ref, pad).astype(jnp.bfloat16)
    tiles = samples // LANES
    for i in range(tiles):
        for j in range(max(i - 1, 0), min(i + 2, tiles)):
            fir[LANES * i : LANES * (i + 1), LANES * j : LANES * (j + 1)] = three[
                :, LANES * (j - i + 1) : LANES * (j - i + 2)
            ]
    copies[2].wait()
    both_tables = jnp.dot(fir[...], dft_ref[...], preferred_element_type=jnp.float32).astype(
        jnp.bfloat16
    )
    copies[1].wait()
    for load in loads:
        load.wait()
    spectra, both = [], []
    for b in range(blocks):
        block = rec_ref[b].reshape(windows * width, samples)
        spectra.append(jnp.dot(block, both_tables, preferred_element_type=jnp.float32))
    for b in range(blocks):
        re, im = spectra[b][:, :LANES], spectra[b][:, LANES:]
        amp = jnp.sqrt(re * re + im * im)
        high = amp.astype(jnp.bfloat16)
        low = (amp - high.astype(jnp.float32)).astype(jnp.bfloat16)
        both.append(
            jnp.dot(
                jnp.concatenate([high, low], axis=1), gather, preferred_element_type=jnp.float32
            )
        )
    for b in range(blocks):
        smooth = both[b][:, :LANES] * (1.0 / 5.0)
        mean_amp = both[b][:, LANES:] * (1.0 / BINS) + 1e-06
        scale = 1.0 / jnp.maximum(smooth, 0.5 * mean_amp)
        for which in range(2):
            value = spectra[b][:, LANES * which : LANES * (which + 1)]
            unit = (value * scale).astype(jnp.bfloat16)
            white[which, b] = unit.reshape(windows, width, LANES)
            sums[which, b] = jnp.sum(
                unit.astype(jnp.float32).reshape(windows, width, LANES), axis=1
            )

    def cross(k):
        b = relative(lax.axis_index("chan"), k, blocks)
        re, im = [], []
        for s in range(count):
            total_re = jnp.zeros((width, LANES), jnp.float32)
            total_im = jnp.zeros((width, LANES), jnp.float32)
            for w in range(windows):
                src_re = sums[0, ids_ref[s], w : w + 1, :]
                src_im = sums[1, ids_ref[s], w : w + 1, :]
                white_re = white[0, b, w].astype(jnp.float32)
                white_im = white[1, b, w].astype(jnp.float32)
                total_re += white_re * src_re + white_im * src_im
                total_im += white_im * src_re - white_re * src_im
            re.append(total_re)
            im.append(total_im)
        return pack(re, im).astype(jnp.bfloat16)

    whole, shared = kinds(blocks)
    half = width // 2
    first = lax.axis_index("rep") == 0
    for i, k in enumerate(whole):
        out_ref[width * i : width * (i + 1), :] = cross(k)
    for i, k in enumerate(shared):
        start = width * len(whole) + half * i
        value = cross(k)
        top, bottom = value[:half], value[half:]
        out_ref[start : start + half, :] = jnp.where(first, bottom, top)
        kept_ref[half * i : half * (i + 1), :] = jnp.where(first, top, bottom)


def kinds(blocks):
    return list(range(1, blocks // 2)), list(range(blocks // 2, blocks)) + [0]


def relative(me, k, size):
    return (me + k) % size


def local_cross(source_ids, records, taps, dft):
    windows, channels, samples = records.shape
    blocks = channels // BLOCK
    whole, shared = (len(kind) for kind in kinds(blocks))
    half = BLOCK // 2
    hbm = pl.BlockSpec(memory_space=pltpu.HBM)
    return pl.pallas_call(
        spectra_kernel,
        out_shape=[
            jax.ShapeDtypeStruct((BLOCK * whole + half * shared, 6 * LANES), jnp.bfloat16),
            jax.ShapeDtypeStruct((half * shared, 6 * LANES), jnp.bfloat16),
        ],
        in_specs=[hbm] * 4,
        out_specs=[pl.BlockSpec(memory_space=pltpu.VMEM)] * 2,
        scratch_shapes=[
            pltpu.SMEM(source_ids.shape, jnp.int32),
            pltpu.VMEM((blocks, windows, BLOCK, samples), jnp.bfloat16),
            pltpu.VMEM(taps.shape, jnp.float32),
            pltpu.VMEM(dft.shape, jnp.bfloat16),
            pltpu.VMEM((8, LANES), jnp.float32),
            pltpu.VMEM((samples, samples), jnp.bfloat16),
            pltpu.VMEM((2, blocks, windows, BLOCK, LANES), jnp.bfloat16),
            pltpu.VMEM((2, blocks, windows, LANES), jnp.float32),
            pltpu.SemaphoreType.DMA((2,)),
            pltpu.SemaphoreType.DMA,
            pltpu.SemaphoreType.DMA((blocks,)),
        ],
        compiler_params=pltpu.CompilerParams(vmem_limit_bytes=VMEM_LIMIT),
    )(*(pltpu.with_memory_space_constraint(v, pltpu.HBM) for v in (source_ids, records, taps, dft)))


def tree(values):
    while len(values) > 1:
        values = [sum(values[i + 1 : i + 2], values[i]) for i in range(0, len(values), 2)]
    return values[0]


def add_kernel(whole, own, kept, other, *outs):
    rows = outs[0].shape[0]
    for i, out in enumerate(outs):
        if i < whole:
            at = slice(rows * i, rows * (i + 1))
            mine = own[at, :]
        else:
            half = out.shape[0]
            mine = kept[half * (i - whole) : half * (i - whole + 1), :]
            start = rows * whole + half * (i - whole)
            at = slice(start, start + half)
        total = mine.astype(jnp.float32) + other[at, :].astype(jnp.float32)
        out[...] = total.astype(out.dtype)


def tree_kernel(*refs):
    refs[-1][...] = tree([ref[...].astype(jnp.float32) for ref in refs[:-1]]).astype(refs[-1].dtype)


def core_kernel(turns, shares, *refs):
    out = refs[-1]
    arrived = [ref[...].astype(jnp.float32) for ref in refs[:-1]]
    share, arrived = tree(arrived[:shares]), arrived[shares:]
    blocks = [tree(arrived[i : i + turns]) for i in range(0, len(arrived), turns)]
    total = functools.reduce(jnp.add, blocks)
    rows = total.shape[0]
    out[:rows, :] = total.astype(out.dtype)
    out[rows:, :] = share.astype(out.dtype)


def lag_kernel(scale, table_ref, own, other, out):
    rows = out.shape[1]
    first = lax.axis_index("rep") == 0
    mine, theirs = own[rows:, :].astype(jnp.float32), other[rows:, :].astype(jnp.float32)
    shares = jnp.concatenate(
        [jnp.where(first, mine, theirs), jnp.where(first, theirs, mine)], axis=0
    )
    total = own[:rows, :].astype(jnp.float32) + other[:rows, :].astype(jnp.float32) + shares
    cross = unpack(total)
    high = cross.astype(jnp.bfloat16)
    low = (cross - high.astype(jnp.float32)).astype(jnp.bfloat16)
    dot = functools.partial(jnp.dot, preferred_element_type=jnp.float32)
    top, bottom = table_ref[: 2 * LANES, :], table_ref[2 * LANES :, :]
    lags = dot(high, top) + (dot(low, top) + dot(high, bottom))
    out[...] = (scale * lags).reshape(out.shape)


def in_vmem(kernel, out_shape, inputs):
    vmem = pl.BlockSpec(memory_space=pltpu.VMEM)
    several = isinstance(out_shape, list)
    return pl.pallas_call(
        kernel,
        out_shape=out_shape,
        in_specs=[vmem] * len(inputs),
        out_specs=[vmem] * len(out_shape) if several else vmem,
        compiler_params=pltpu.CompilerParams(vmem_limit_bytes=VMEM_LIMIT),
    )(*inputs)


def body(records, fir_taps, source_ids):
    samples = records.shape[2]
    chans, times, cores = (lax.axis_size(axis) for axis in ("chan", "tm", "rep"))
    assert cores == 2 and times & (times - 1) == 0
    axes = ("chan", "tm", "rep")
    devices = [(a, t, r) for a in range(chans) for t in range(times) for r in range(cores)]
    number = {device: i for i, device in enumerate(devices)}

    def send(value, to):
        return lax.ppermute(value, axes, [(number[d], number[to(*d)]) for d in devices])

    own, kept = local_cross(
        source_ids, records, fir_taps.reshape(1, -1), jnp.asarray(dft_table(samples))
    )
    width, half = 6 * LANES, BLOCK // 2
    whole, shared = kinds(chans)
    other = send(own, lambda a, t, r: (a, t, 1 - r))
    full = jax.ShapeDtypeStruct((BLOCK, width), jnp.bfloat16)
    part = jax.ShapeDtypeStruct((half, width), jnp.bfloat16)
    pieces = in_vmem(
        functools.partial(add_kernel, len(whole)),
        [full] * len(whole) + [part] * len(shared),
        [own, kept, other],
    )
    shares = [
        send(piece, lambda a, t, r, k=k: (relative(a, k, chans), t, r))
        for k, piece in zip(shared[:-1], pieces[len(whole) :])
    ]
    arrived = [
        send(piece, lambda a, t, r, k=k: (relative(a, k, chans), t ^ (turn + r), r))
        for k, piece in zip(whole, pieces)
        for turn in range(0, times, cores)
    ]
    share = in_vmem(tree_kernel, part, [pieces[-1]] + shares)
    shares = [share] + [
        send(share, lambda a, t, r, j=j: (a, t ^ j, r)) for j in range(1, times)
    ]
    total = in_vmem(
        functools.partial(core_kernel, -(-times // cores), times),
        jax.ShapeDtypeStruct((BLOCK + half, width), jnp.bfloat16),
        shares + arrived,
    )
    other = send(total, lambda a, t, r: (a, t, 1 - r))
    windows_all = records.shape[0] * chans * times * cores
    scale = 1.0 / math.sqrt(windows_all * BLOCK * BINS)
    return in_vmem(
        functools.partial(lag_kernel, scale),
        jax.ShapeDtypeStruct((source_ids.shape[0], BLOCK, LAGS), jnp.float32),
        [jnp.asarray(lag_table(samples)), total, other],
    )


def solution(mesh):
    in_specs = (P(("chan", "tm", "rep"), "parts", None), P(), P("parts"))
    out_specs = P(None, ("parts", "chan"), None)
    return jax.shard_map(body, mesh=mesh, in_specs=in_specs, out_specs=out_specs, check_vma=False)
```

```python
import functools
import math

import jax
import jax.numpy as jnp
import numpy as np
from jax import lax
from jax.experimental import pallas as pl
from jax.experimental.pallas import tpu as pltpu
from jax.sharding import PartitionSpec as P

BINS = 96
LAGS = 256
BLOCK = 64
LANES = 128
VMEM_LIMIT = 32 * 1024 * 1024


def dft_table(samples):
    times = np.arange(samples)[:, None]
    freqs = np.arange(1, BINS + 1)[None, :]
    angle = np.float32(2.0 * math.pi / samples) * (times * freqs % samples).astype(np.float32)
    table = np.zeros((samples, 2 * LANES), np.float32)
    table[:, :BINS] = np.cos(angle)
    table[:, LANES : LANES + BINS] = -np.sin(angle)
    return table.astype(jnp.bfloat16)


def lag_table(samples):
    freqs = np.arange(1, BINS + 1)[:, None]
    shifts = np.arange(LAGS)[None, :] - LAGS // 2
    angle = np.float32(2.0 * math.pi / samples) * np.mod(freqs * shifts, samples).astype(np.float32)
    table = np.zeros((2 * LANES, LAGS), np.float32)
    table[:BINS] = np.cos(angle)
    table[LANES : LANES + BINS] = -np.sin(angle)
    high = table.astype(jnp.bfloat16)
    low = (table - high.astype(np.float32)).astype(jnp.bfloat16)
    return np.concatenate([high, low], axis=0)


def fir_blocks(taps_ref, pad_ref):
    taps = taps_ref.shape[1]
    half = taps // 2
    pad_ref[...] = jnp.zeros(pad_ref.shape, jnp.float32)
    pad_ref[0:1, 0:taps] = taps_ref[...]
    rows = lax.broadcasted_iota(jnp.int32, (LANES, LANES), 0)
    cols = lax.broadcasted_iota(jnp.int32, (LANES, LANES), 1)
    flip = (rows + cols == taps - 1).astype(jnp.bfloat16)
    turned = jnp.dot(
        pad_ref[...].astype(jnp.bfloat16), flip, preferred_element_type=jnp.float32
    )[0:1]
    wide = jnp.concatenate([turned, jnp.zeros((1, 2 * LANES), jnp.float32)], axis=1)
    wide = jnp.broadcast_to(wide, (LANES, 3 * LANES))
    return pltpu.roll(wide, LANES - half, 1, stride=1, stride_axis=0)


def pack(re, im):
    lane = lax.broadcasted_iota(jnp.int32, re[0].shape, 1)
    tiles = []
    for index in range(3):
        for part, last in ((re[index], re[3]), (im[index], im[3])):
            moved = pltpu.roll(last, BINS - 32 * index, 1)
            tiles.append(jnp.where(lane < BINS, part, moved))
    return jnp.concatenate(tiles, axis=1)


def unpack(packed):
    lane = lax.broadcasted_iota(jnp.int32, (packed.shape[0], LANES), 1)
    tiles = [packed[:, LANES * i : LANES * (i + 1)] for i in range(6)]
    last = []
    for which in range(2):
        total = jnp.zeros_like(tiles[0])
        for index in range(3):
            moved = pltpu.roll(tiles[2 * index + which], LANES - BINS + 32 * index, 1)
            total = jnp.where((lane >= 32 * index) & (lane < 32 * index + 32), moved, total)
        last.append(total)
    rows = [jnp.concatenate([tiles[2 * i], tiles[2 * i + 1]], axis=1) for i in range(3)]
    return jnp.concatenate(rows + [jnp.concatenate(last, axis=1)], axis=0)


def spectra_kernel(
    ids_hbm,
    rec_hbm,
    taps_hbm,
    dft_hbm,
    out_ref,
    kept_ref,
    ids_ref,
    rec_ref,
    taps_ref,
    dft_ref,
    pad,
    fir,
    white,
    sums,
    small_sems,
    dft_sem,
    rec_sems,
):
    blocks, windows, width, samples = rec_ref.shape
    count = ids_ref.shape[0]
    copies = [
        pltpu.make_async_copy(taps_hbm, taps_ref, small_sems.at[0]),
        pltpu.make_async_copy(ids_hbm, ids_ref, small_sems.at[1]),
        pltpu.make_async_copy(dft_hbm, dft_ref, dft_sem),
    ]
    for copy in copies:
        copy.start()
    loads = [
        pltpu.make_async_copy(
            rec_hbm.at[:, pl.ds(width * b, width), :], rec_ref.at[b], rec_sems.at[b]
        )
        for b in range(blocks)
    ]
    for load in loads:
        load.start()
    fir[...] = jnp.zeros(fir.shape, fir.dtype)
    rows = lax.broadcasted_iota(jnp.int32, (2 * LANES, 2 * LANES), 0) % LANES
    cols = lax.broadcasted_iota(jnp.int32, (2 * LANES, 2 * LANES), 1)
    near = (jnp.abs(rows - cols) <= 2) | (cols >= LANES)
    gather = jnp.where(near, 1.0, 0.0).astype(jnp.bfloat16)
    copies[0].wait()
    three = fir_blocks(taps_ref, pad).astype(jnp.bfloat16)
    tiles = samples // LANES
    for i in range(tiles):
        for j in range(max(i - 1, 0), min(i + 2, tiles)):
            fir[LANES * i : LANES * (i + 1), LANES * j : LANES * (j + 1)] = three[
                :, LANES * (j - i + 1) : LANES * (j - i + 2)
            ]
    copies[2].wait()
    copies[1].wait()
    for load in loads:
        load.wait()
    filtered, spectra, both = [], [], []
    for b in range(blocks):
        block = rec_ref[b].reshape(windows * width, samples)
        filtered.append(
            jnp.dot(block, fir[...], preferred_element_type=jnp.float32).astype(jnp.bfloat16)
        )
    for b in range(blocks):
        spectra.append(jnp.dot(filtered[b], dft_ref[...], preferred_element_type=jnp.float32))
    for b in range(blocks):
        re, im = spectra[b][:, :LANES], spectra[b][:, LANES:]
        amp = jnp.sqrt(re * re + im * im)
        high = amp.astype(jnp.bfloat16)
        low = (amp - high.astype(jnp.float32)).astype(jnp.bfloat16)
        both.append(
            jnp.dot(
                jnp.concatenate([high, low], axis=1), gather, preferred_element_type=jnp.float32
            )
        )
    for b in range(blocks):
        smooth = both[b][:, :LANES] * (1.0 / 5.0)
        mean_amp = both[b][:, LANES:] * (1.0 / BINS) + 1e-06
        scale = 1.0 / jnp.maximum(smooth, 0.5 * mean_amp)
        for which in range(2):
            value = spectra[b][:, LANES * which : LANES * (which + 1)]
            unit = (value * scale).astype(jnp.bfloat16)
            white[which, b] = unit.reshape(windows, width, LANES)
            sums[which, b] = jnp.sum(
                unit.astype(jnp.float32).reshape(windows, width, LANES), axis=1
            )

    def cross(k):
        b = relative(lax.axis_index("chan"), k, blocks)
        re, im = [], []
        for s in range(count):
            total_re = jnp.zeros((width, LANES), jnp.float32)
            total_im = jnp.zeros((width, LANES), jnp.float32)
            for w in range(windows):
                src_re = sums[0, ids_ref[s], w : w + 1, :]
                src_im = sums[1, ids_ref[s], w : w + 1, :]
                white_re = white[0, b, w].astype(jnp.float32)
                white_im = white[1, b, w].astype(jnp.float32)
                total_re += white_re * src_re + white_im * src_im
                total_im += white_im * src_re - white_re * src_im
            re.append(total_re)
            im.append(total_im)
        return pack(re, im).astype(jnp.bfloat16)

    whole, shared = kinds(blocks)
    half = width // 2
    first = lax.axis_index("rep") == 0
    for i, k in enumerate(whole):
        out_ref[width * i : width * (i + 1), :] = cross(k)
    for i, k in enumerate(shared):
        start = width * len(whole) + half * i
        value = cross(k)
        top, bottom = value[:half], value[half:]
        out_ref[start : start + half, :] = jnp.where(first, bottom, top)
        kept_ref[half * i : half * (i + 1), :] = jnp.where(first, top, bottom)


def kinds(blocks):
    return list(range(1, blocks // 2)), list(range(blocks // 2, blocks)) + [0]


def relative(me, k, size):
    return (me + k) % size


def local_cross(source_ids, records, taps, dft):
    windows, channels, samples = records.shape
    blocks = channels // BLOCK
    whole, shared = (len(kind) for kind in kinds(blocks))
    half = BLOCK // 2
    hbm = pl.BlockSpec(memory_space=pltpu.HBM)
    return pl.pallas_call(
        spectra_kernel,
        out_shape=[
            jax.ShapeDtypeStruct((BLOCK * whole + half * shared, 6 * LANES), jnp.bfloat16),
            jax.ShapeDtypeStruct((half * shared, 6 * LANES), jnp.bfloat16),
        ],
        in_specs=[hbm] * 4,
        out_specs=[pl.BlockSpec(memory_space=pltpu.VMEM)] * 2,
        scratch_shapes=[
            pltpu.SMEM(source_ids.shape, jnp.int32),
            pltpu.VMEM((blocks, windows, BLOCK, samples), jnp.bfloat16),
            pltpu.VMEM(taps.shape, jnp.float32),
            pltpu.VMEM(dft.shape, jnp.bfloat16),
            pltpu.VMEM((8, LANES), jnp.float32),
            pltpu.VMEM((samples, samples), jnp.bfloat16),
            pltpu.VMEM((2, blocks, windows, BLOCK, LANES), jnp.bfloat16),
            pltpu.VMEM((2, blocks, windows, LANES), jnp.float32),
            pltpu.SemaphoreType.DMA((2,)),
            pltpu.SemaphoreType.DMA,
            pltpu.SemaphoreType.DMA((blocks,)),
        ],
        compiler_params=pltpu.CompilerParams(vmem_limit_bytes=VMEM_LIMIT),
    )(*(pltpu.with_memory_space_constraint(v, pltpu.HBM) for v in (source_ids, records, taps, dft)))


def tree(values):
    while len(values) > 1:
        values = [sum(values[i + 1 : i + 2], values[i]) for i in range(0, len(values), 2)]
    return values[0]


def add_kernel(whole, own, kept, other, *outs):
    rows = outs[0].shape[0]
    for i, out in enumerate(outs):
        if i < whole:
            at = slice(rows * i, rows * (i + 1))
            mine = own[at, :]
        else:
            half = out.shape[0]
            mine = kept[half * (i - whole) : half * (i - whole + 1), :]
            start = rows * whole + half * (i - whole)
            at = slice(start, start + half)
        total = mine.astype(jnp.float32) + other[at, :].astype(jnp.float32)
        out[...] = total.astype(out.dtype)


def tree_kernel(*refs):
    refs[-1][...] = tree([ref[...].astype(jnp.float32) for ref in refs[:-1]]).astype(refs[-1].dtype)


def core_kernel(turns, shares, *refs):
    out = refs[-1]
    arrived = [ref[...].astype(jnp.float32) for ref in refs[:-1]]
    share, arrived = tree(arrived[:shares]), arrived[shares:]
    blocks = [tree(arrived[i : i + turns]) for i in range(0, len(arrived), turns)]
    total = functools.reduce(jnp.add, blocks)
    rows = total.shape[0]
    out[:rows, :] = total.astype(out.dtype)
    out[rows:, :] = share.astype(out.dtype)


def lag_kernel(scale, table_ref, own, other, out):
    rows = out.shape[1]
    first = lax.axis_index("rep") == 0
    mine, theirs = own[rows:, :].astype(jnp.float32), other[rows:, :].astype(jnp.float32)
    shares = jnp.concatenate(
        [jnp.where(first, mine, theirs), jnp.where(first, theirs, mine)], axis=0
    )
    total = own[:rows, :].astype(jnp.float32) + other[:rows, :].astype(jnp.float32) + shares
    cross = unpack(total)
    high = cross.astype(jnp.bfloat16)
    low = (cross - high.astype(jnp.float32)).astype(jnp.bfloat16)
    dot = functools.partial(jnp.dot, preferred_element_type=jnp.float32)
    top, bottom = table_ref[: 2 * LANES, :], table_ref[2 * LANES :, :]
    lags = dot(high, top) + (dot(low, top) + dot(high, bottom))
    out[...] = (scale * lags).reshape(out.shape)


def in_vmem(kernel, out_shape, inputs):
    vmem = pl.BlockSpec(memory_space=pltpu.VMEM)
    several = isinstance(out_shape, list)
    return pl.pallas_call(
        kernel,
        out_shape=out_shape,
        in_specs=[vmem] * len(inputs),
        out_specs=[vmem] * len(out_shape) if several else vmem,
        compiler_params=pltpu.CompilerParams(vmem_limit_bytes=VMEM_LIMIT),
    )(*inputs)


def body(records, fir_taps, source_ids):
    samples = records.shape[2]
    chans, times, cores = (lax.axis_size(axis) for axis in ("chan", "tm", "rep"))
    assert cores == 2 and times & (times - 1) == 0
    axes = ("chan", "tm", "rep")
    devices = [(a, t, r) for a in range(chans) for t in range(times) for r in range(cores)]
    number = {device: i for i, device in enumerate(devices)}

    def send(value, to):
        return lax.ppermute(value, axes, [(number[d], number[to(*d)]) for d in devices])

    own, kept = local_cross(
        source_ids, records, fir_taps.reshape(1, -1), jnp.asarray(dft_table(samples))
    )
    width, half = 6 * LANES, BLOCK // 2
    whole, shared = kinds(chans)
    other = send(own, lambda a, t, r: (a, t, 1 - r))
    full = jax.ShapeDtypeStruct((BLOCK, width), jnp.bfloat16)
    part = jax.ShapeDtypeStruct((half, width), jnp.bfloat16)
    pieces = in_vmem(
        functools.partial(add_kernel, len(whole)),
        [full] * len(whole) + [part] * len(shared),
        [own, kept, other],
    )
    shares = [
        send(piece, lambda a, t, r, k=k: (relative(a, k, chans), t, r))
        for k, piece in zip(shared[:-1], pieces[len(whole) :])
    ]
    arrived = [
        send(piece, lambda a, t, r, k=k: (relative(a, k, chans), t ^ (turn + r), r))
        for k, piece in zip(whole, pieces)
        for turn in range(0, times, cores)
    ]
    share = in_vmem(tree_kernel, part, [pieces[-1]] + shares)
    shares = [share] + [
        send(share, lambda a, t, r, j=j: (a, t ^ j, r)) for j in range(1, times)
    ]
    total = in_vmem(
        functools.partial(core_kernel, -(-times // cores), times),
        jax.ShapeDtypeStruct((BLOCK + half, width), jnp.bfloat16),
        shares + arrived,
    )
    other = send(total, lambda a, t, r: (a, t, 1 - r))
    windows_all = records.shape[0] * chans * times * cores
    scale = 1.0 / math.sqrt(windows_all * BLOCK * BINS)
    return in_vmem(
        functools.partial(lag_kernel, scale),
        jax.ShapeDtypeStruct((source_ids.shape[0], BLOCK, LAGS), jnp.float32),
        [jnp.asarray(lag_table(samples)), total, other],
    )


def solution(mesh):
    in_specs = (P(("chan", "tm", "rep"), "parts", None), P(), P("parts"))
    out_specs = P(None, ("parts", "chan"), None)
    return jax.shard_map(body, mesh=mesh, in_specs=in_specs, out_specs=out_specs, check_vma=False)
```

```python
import functools
import math

import jax
import jax.numpy as jnp
import numpy as np
from jax import lax
from jax.experimental import pallas as pl
from jax.experimental.pallas import tpu as pltpu
from jax.sharding import PartitionSpec as P

BINS = 96
LAGS = 256
BLOCK = 64
LANES = 128
VMEM_LIMIT = 32 * 1024 * 1024


def dft_table(samples):
    times = np.arange(samples)[:, None]
    freqs = np.arange(1, BINS + 1)[None, :]
    angle = np.float32(2.0 * math.pi / samples) * (times * freqs % samples).astype(np.float32)
    table = np.zeros((samples, 2 * LANES), np.float32)
    table[:, :BINS] = np.cos(angle)
    table[:, LANES : LANES + BINS] = -np.sin(angle)
    return table.astype(jnp.bfloat16)


def lag_table(samples):
    freqs = np.arange(1, BINS + 1)[:, None]
    shifts = np.arange(LAGS)[None, :] - LAGS // 2
    angle = np.float32(2.0 * math.pi / samples) * np.mod(freqs * shifts, samples).astype(np.float32)
    table = np.zeros((2 * LANES, LAGS), np.float32)
    table[:BINS] = np.cos(angle)
    table[LANES : LANES + BINS] = -np.sin(angle)
    high = table.astype(jnp.bfloat16)
    low = (table - high.astype(np.float32)).astype(jnp.bfloat16)
    return np.concatenate([high, low], axis=0)


def fir_blocks(taps_ref, pad_ref):
    taps = taps_ref.shape[1]
    half = taps // 2
    pad_ref[...] = jnp.zeros(pad_ref.shape, jnp.float32)
    pad_ref[0:1, 0:taps] = taps_ref[...]
    rows = lax.broadcasted_iota(jnp.int32, (LANES, LANES), 0)
    cols = lax.broadcasted_iota(jnp.int32, (LANES, LANES), 1)
    flip = (rows + cols == taps - 1).astype(jnp.bfloat16)
    turned = jnp.dot(
        pad_ref[...].astype(jnp.bfloat16), flip, preferred_element_type=jnp.float32
    )[0:1]
    wide = jnp.concatenate([turned, jnp.zeros((1, 2 * LANES), jnp.float32)], axis=1)
    wide = jnp.broadcast_to(wide, (LANES, 3 * LANES))
    return pltpu.roll(wide, LANES - half, 1, stride=1, stride_axis=0)


def pack(re, im):
    lane = lax.broadcasted_iota(jnp.int32, re[0].shape, 1)
    tiles = []
    for index in range(3):
        for part, last in ((re[index], re[3]), (im[index], im[3])):
            moved = pltpu.roll(last, BINS - 32 * index, 1)
            tiles.append(jnp.where(lane < BINS, part, moved))
    return jnp.concatenate(tiles, axis=1)


def unpack(packed):
    lane = lax.broadcasted_iota(jnp.int32, (packed.shape[0], LANES), 1)
    tiles = [packed[:, LANES * i : LANES * (i + 1)] for i in range(6)]
    last = []
    for which in range(2):
        total = jnp.zeros_like(tiles[0])
        for index in range(3):
            moved = pltpu.roll(tiles[2 * index + which], LANES - BINS + 32 * index, 1)
            total = jnp.where((lane >= 32 * index) & (lane < 32 * index + 32), moved, total)
        last.append(total)
    rows = [jnp.concatenate([tiles[2 * i], tiles[2 * i + 1]], axis=1) for i in range(3)]
    return jnp.concatenate(rows + [jnp.concatenate(last, axis=1)], axis=0)


def spectra_kernel(
    ids_hbm,
    rec_hbm,
    taps_hbm,
    dft_hbm,
    out_ref,
    kept_ref,
    ids_ref,
    rec_ref,
    taps_ref,
    dft_ref,
    pad,
    fir,
    white,
    sums,
    small_sems,
    dft_sem,
    rec_sems,
):
    blocks, windows, width, samples = rec_ref.shape
    count = ids_ref.shape[0]
    copies = [
        pltpu.make_async_copy(taps_hbm, taps_ref, small_sems.at[0]),
        pltpu.make_async_copy(ids_hbm, ids_ref, small_sems.at[1]),
        pltpu.make_async_copy(dft_hbm, dft_ref, dft_sem),
    ]
    for copy in copies:
        copy.start()
    loads = [
        pltpu.make_async_copy(
            rec_hbm.at[:, pl.ds(width * b, width), :], rec_ref.at[b], rec_sems.at[b]
        )
        for b in range(blocks)
    ]
    for load in loads:
        load.start()
    fir[...] = jnp.zeros(fir.shape, fir.dtype)
    rows = lax.broadcasted_iota(jnp.int32, (2 * LANES, 2 * LANES), 0) % LANES
    cols = lax.broadcasted_iota(jnp.int32, (2 * LANES, 2 * LANES), 1)
    near = (jnp.abs(rows - cols) <= 2) | (cols >= LANES)
    gather = jnp.where(near, 1.0, 0.0).astype(jnp.bfloat16)
    copies[0].wait()
    three = fir_blocks(taps_ref, pad).astype(jnp.bfloat16)
    tiles = samples // LANES
    for i in range(tiles):
        for j in range(max(i - 1, 0), min(i + 2, tiles)):
            fir[LANES * i : LANES * (i + 1), LANES * j : LANES * (j + 1)] = three[
                :, LANES * (j - i + 1) : LANES * (j - i + 2)
            ]
    copies[2].wait()
    copies[1].wait()
    for load in loads:
        load.wait()
    filtered, spectra, both = [], [], []
    for b in range(blocks):
        block = rec_ref[b].reshape(windows * width, samples)
        filtered.append(
            jnp.dot(block, fir[...], preferred_element_type=jnp.float32).astype(jnp.bfloat16)
        )
    for b in range(blocks):
        spectra.append(jnp.dot(filtered[b], dft_ref[...], preferred_element_type=jnp.float32))
    for b in range(blocks):
        re, im = spectra[b][:, :LANES], spectra[b][:, LANES:]
        amp = jnp.sqrt(re * re + im * im)
        high = amp.astype(jnp.bfloat16)
        low = (amp - high.astype(jnp.float32)).astype(jnp.bfloat16)
        both.append(
            jnp.dot(
                jnp.concatenate([high, low], axis=1), gather, preferred_element_type=jnp.float32
            )
        )
    for b in range(blocks):
        smooth = both[b][:, :LANES] * (1.0 / 5.0)
        mean_amp = both[b][:, LANES:] * (1.0 / BINS) + 1e-06
        scale = 1.0 / jnp.maximum(smooth, 0.5 * mean_amp)
        for which in range(2):
            value = spectra[b][:, LANES * which : LANES * (which + 1)]
            unit = (value * scale).astype(jnp.bfloat16)
            white[which, b] = unit.reshape(windows, width, LANES)
            sums[which, b] = jnp.sum(
                unit.astype(jnp.float32).reshape(windows, width, LANES), axis=1
            )

    def cross(k):
        b = relative(lax.axis_index("chan"), k, blocks)
        re, im = [], []
        for s in range(count):
            total_re = jnp.zeros((width, LANES), jnp.float32)
            total_im = jnp.zeros((width, LANES), jnp.float32)
            for w in range(windows):
                src_re = sums[0, ids_ref[s], w : w + 1, :]
                src_im = sums[1, ids_ref[s], w : w + 1, :]
                white_re = white[0, b, w].astype(jnp.float32)
                white_im = white[1, b, w].astype(jnp.float32)
                total_re += white_re * src_re + white_im * src_im
                total_im += white_im * src_re - white_re * src_im
            re.append(total_re)
            im.append(total_im)
        return pack(re, im).astype(jnp.bfloat16)

    whole, shared = kinds(blocks)
    half = width // 2
    first = lax.axis_index("rep") == 0
    for i, k in enumerate(whole):
        out_ref[width * i : width * (i + 1), :] = cross(k)
    for i, k in enumerate(shared):
        start = width * len(whole) + half * i
        value = cross(k)
        top, bottom = value[:half], value[half:]
        upper = first if k else ~first
        out_ref[start : start + half, :] = jnp.where(upper, bottom, top)
        kept_ref[half * i : half * (i + 1), :] = jnp.where(upper, top, bottom)


def kinds(blocks):
    return list(range(3 * blocks // 4 - 1, 0, -1)), list(range(3 * blocks // 4, blocks)) + [0]


def relative(me, k, size):
    half = size // 2
    if k < half:
        return me ^ k
    low = (me < half) * 1
    return low * (half + (me + k) % half) + (1 - low) * ((size - 1 - me + k) % half)


def local_cross(source_ids, records, taps, dft):
    windows, channels, samples = records.shape
    blocks = channels // BLOCK
    whole, shared = (len(kind) for kind in kinds(blocks))
    half = BLOCK // 2
    hbm = pl.BlockSpec(memory_space=pltpu.HBM)
    return pl.pallas_call(
        spectra_kernel,
        out_shape=[
            jax.ShapeDtypeStruct((BLOCK * whole + half * shared, 6 * LANES), jnp.bfloat16),
            jax.ShapeDtypeStruct((half * shared, 6 * LANES), jnp.bfloat16),
        ],
        in_specs=[hbm] * 4,
        out_specs=[pl.BlockSpec(memory_space=pltpu.VMEM)] * 2,
        scratch_shapes=[
            pltpu.SMEM(source_ids.shape, jnp.int32),
            pltpu.VMEM((blocks, windows, BLOCK, samples), jnp.bfloat16),
            pltpu.VMEM(taps.shape, jnp.float32),
            pltpu.VMEM(dft.shape, jnp.bfloat16),
            pltpu.VMEM((8, LANES), jnp.float32),
            pltpu.VMEM((samples, samples), jnp.bfloat16),
            pltpu.VMEM((2, blocks, windows, BLOCK, LANES), jnp.bfloat16),
            pltpu.VMEM((2, blocks, windows, LANES), jnp.float32),
            pltpu.SemaphoreType.DMA((2,)),
            pltpu.SemaphoreType.DMA,
            pltpu.SemaphoreType.DMA((blocks,)),
        ],
        compiler_params=pltpu.CompilerParams(vmem_limit_bytes=VMEM_LIMIT),
    )(*(pltpu.with_memory_space_constraint(v, pltpu.HBM) for v in (source_ids, records, taps, dft)))


def tree(values):
    while len(values) > 1:
        values = [sum(values[i + 1 : i + 2], values[i]) for i in range(0, len(values), 2)]
    return values[0]


def add_kernel(whole, own, kept, other, *outs):
    rows = outs[0].shape[0]
    for i, out in enumerate(outs):
        if i < whole:
            at = slice(rows * i, rows * (i + 1))
            mine = own[at, :]
        else:
            half = out.shape[0]
            mine = kept[half * (i - whole) : half * (i - whole + 1), :]
            start = rows * whole + half * (i - whole)
            at = slice(start, start + half)
        total = mine.astype(jnp.float32) + other[at, :].astype(jnp.float32)
        out[...] = total.astype(out.dtype)


def tree_kernel(*refs):
    refs[-1][...] = tree([ref[...].astype(jnp.float32) for ref in refs[:-1]]).astype(refs[-1].dtype)


def core_kernel(turns, shares, *refs):
    out = refs[-1]
    arrived = [ref[...].astype(jnp.float32) for ref in refs[:-1]]
    share, arrived = tree(arrived[:shares]), arrived[shares:]
    blocks = [tree(arrived[i : i + turns]) for i in range(0, len(arrived), turns)]
    total = functools.reduce(jnp.add, blocks)
    rows = total.shape[0]
    out[:rows, :] = total.astype(out.dtype)
    out[rows:, :] = share.astype(out.dtype)


def lag_kernel(scale, table_ref, own, other, out):
    rows = out.shape[1]
    first = lax.axis_index("rep") == 0
    mine, theirs = own[rows:, :].astype(jnp.float32), other[rows:, :].astype(jnp.float32)
    shares = jnp.concatenate(
        [jnp.where(first, theirs, mine), jnp.where(first, mine, theirs)], axis=0
    )
    total = own[:rows, :].astype(jnp.float32) + other[:rows, :].astype(jnp.float32) + shares
    cross = unpack(total)
    high = cross.astype(jnp.bfloat16)
    low = (cross - high.astype(jnp.float32)).astype(jnp.bfloat16)
    dot = functools.partial(jnp.dot, preferred_element_type=jnp.float32)
    top, bottom = table_ref[: 2 * LANES, :], table_ref[2 * LANES :, :]
    lags = dot(high, top) + (dot(low, top) + dot(high, bottom))
    out[...] = (scale * lags).reshape(out.shape)


def in_vmem(kernel, out_shape, inputs):
    vmem = pl.BlockSpec(memory_space=pltpu.VMEM)
    several = isinstance(out_shape, list)
    return pl.pallas_call(
        kernel,
        out_shape=out_shape,
        in_specs=[vmem] * len(inputs),
        out_specs=[vmem] * len(out_shape) if several else vmem,
        compiler_params=pltpu.CompilerParams(vmem_limit_bytes=VMEM_LIMIT),
    )(*inputs)


def body(records, fir_taps, source_ids):
    samples = records.shape[2]
    chans, times, cores = (lax.axis_size(axis) for axis in ("chan", "tm", "rep"))
    assert cores == 2 and times & (times - 1) == 0
    axes = ("chan", "tm", "rep")
    devices = [(a, t, r) for a in range(chans) for t in range(times) for r in range(cores)]
    number = {device: i for i, device in enumerate(devices)}

    def send(value, to):
        return lax.ppermute(value, axes, [(number[d], number[to(*d)]) for d in devices])

    own, kept = local_cross(
        source_ids, records, fir_taps.reshape(1, -1), jnp.asarray(dft_table(samples))
    )
    width, half = 6 * LANES, BLOCK // 2
    whole, shared = kinds(chans)
    other = send(own, lambda a, t, r: (a, t, 1 - r))
    full = jax.ShapeDtypeStruct((BLOCK, width), jnp.bfloat16)
    part = jax.ShapeDtypeStruct((half, width), jnp.bfloat16)
    pieces = in_vmem(
        functools.partial(add_kernel, len(whole)),
        [full] * len(whole) + [part] * len(shared),
        [own, kept, other],
    )
    shares = [
        send(piece, lambda a, t, r, k=k: (relative(a, k, chans), t, 1 - r))
        for k, piece in zip(shared[:-1], pieces[len(whole) :])
    ]
    arrived = [
        send(piece, lambda a, t, r, k=k: (relative(a, k, chans), t ^ (turn + r), r))
        for k, piece in zip(whole, pieces)
        for turn in range(0, times, cores)
    ]
    share = in_vmem(tree_kernel, part, [pieces[-1]] + shares)
    shares = [share] + [
        send(share, lambda a, t, r, j=j: (a, t ^ j, r)) for j in range(1, times)
    ]
    total = in_vmem(
        functools.partial(core_kernel, -(-times // cores), times),
        jax.ShapeDtypeStruct((BLOCK + half, width), jnp.bfloat16),
        shares + arrived,
    )
    other = send(total, lambda a, t, r: (a, t, 1 - r))
    windows_all = records.shape[0] * chans * times * cores
    scale = 1.0 / math.sqrt(windows_all * BLOCK * BINS)
    return in_vmem(
        functools.partial(lag_kernel, scale),
        jax.ShapeDtypeStruct((source_ids.shape[0], BLOCK, LAGS), jnp.float32),
        [jnp.asarray(lag_table(samples)), total, other],
    )


def solution(mesh):
    in_specs = (P(("chan", "tm", "rep"), "parts", None), P(), P("parts"))
    out_specs = P(None, ("parts", "chan"), None)
    return jax.shard_map(body, mesh=mesh, in_specs=in_specs, out_specs=out_specs, check_vma=False)
```
